256 devices in a mesh: space: 32 (over z_lo, y, core), mem: 8 (over z_hi, x).
Axes of the slice: x: 4, y: 4, z: 8 (z_hi: 2, z_lo: 4; z = z_hi * 4 + z_lo), core: 2. Of those that a mesh axis runs over, the one named last changes fastest.
Arguments:
- control: bfloat16 [56, 8, 1024, 256], P('mem', None, 'space'), may hold values from -6 to 6
- ensemble: bfloat16 [56, 8, 256, 1024], P('mem', None, 'space'), may hold values from -0.75 to 0.75
- innovation: float32 [8, 256, 1024], P(None, 'space'), may hold values from -6 to 6
- precision_obs: float32 [8, 256, 1024], P(None, 'space'), may hold values from 1 to 4
- classes_x: int32 [2], replicated, may hold values from 0 to 7
- classes_y: int32 [8], replicated, may hold values from 0 to 7
- tables_x: bfloat16 [8, 5, 128, 128], replicated, may hold values from -0.5 to 2, as said below
- tables_y: bfloat16 [8, 5, 128, 128], replicated, may hold values from -0.5 to 2, as said below
Outputs:
- increment: float32 [8, 256, 1024], P('mem', 'space')
- gradient: bfloat16 [56, 8, 1024, 256], P('mem', None, 'space')
The draws below stay inside these ranges and needn't reach their ends.
Inputs may be any that keep to these rules, and one draw needn't show every extreme that they name: `tables_x`: blocks of the banded filter matrices of each scale class. `tables_y`: blocks of the banded filter matrices of each scale class.
All inputs are finite; a program needn't handle non-finite values.
Results may differ from the reference program's by a relative error of at most 0.0056.
Values may be sent and summed in bfloat16 or wider, within the bound.
A program may use at most 64 MiB of HBM per device.

```python
import math
import jax
import jax.numpy as jnp
from jax import lax

LEVELS = 8
BLOCK = 128
BANDS = 5
CLASSES = 8
MEMBERS = 56
NX = 256
NY = 1024


def draw_filter(key):
    key_diag, key_off = jax.random.split(key)
    spread = 0.5 / jnp.sqrt(jnp.float32(BANDS * BLOCK))
    diag_vals = jax.random.uniform(key_diag, (CLASSES, BLOCK), jnp.float32, 0.6, 1.4)
    off_vals = jnp.clip(jax.random.normal(key_off, (CLASSES, BANDS, BLOCK, BLOCK), jnp.float32), -4.0, 4.0) * spread
    identity = jnp.eye(BLOCK, dtype=jnp.float32)
    centre = (jnp.arange(BANDS) == (BANDS - 1) // 2).astype(jnp.float32)
    diagonal = centre[None, :, None, None] * identity[None, None, :, :] * diag_vals[:, None, :, None]
    return (off_vals + diagonal).astype(jnp.bfloat16)


def draw_tables_x(key, part):
    key = jax.random.fold_in(key, 11)
    return draw_filter(key)


def draw_tables_y(key, part):
    key = jax.random.fold_in(key, 23)
    return draw_filter(key)


def plant(values, stream_key, smallest, top_value):
    place = [jax.random.randint(jax.random.fold_in(stream_key, axis), (), 0, length) for axis, length in enumerate(values.shape)]
    widest = values.shape.index(max(values.shape))
    next_to = place[:widest] + [(place[widest] + 1) % values.shape[widest]] + place[widest + 1:]
    return values.at[tuple(place)].set(smallest).at[tuple(next_to)].set(top_value)


def shard_levels(key, dims, cuts, smallest, high):
    gain, own = 1.0, jax.random.fold_in(key, 6)
    for axis_at, shards_of in cuts:
        draws = jnp.exp(jax.random.uniform(jax.random.fold_in(own, axis_at), (shards_of,), jnp.float32, smallest / len(cuts), high / len(cuts)))
        gain = gain * jnp.repeat(draws, dims[axis_at] // shards_of).reshape([-1 if axis == axis_at else 1 for axis in range(len(dims))])
    return gain


def bell_draw(stream_key, dims, scale, bound, cuts=(), held_as=jnp.bfloat16):
    drawn = scale * jax.random.normal(stream_key, dims, jnp.float32)
    if cuts:
        drawn = drawn * shard_levels(stream_key, dims, cuts, -0.22, 0.18)
    return jnp.clip(drawn, -bound, bound).astype(held_as)


def setup_inputs(seed: int = 0) -> dict:
    key_list = jax.random.split(jax.random.key(seed), 9)
    control = bell_draw(key_list[0], (MEMBERS, LEVELS, NY, NX), 1.0, 6.0, ((0, 8), (2, 32)))
    ensemble = bell_draw(key_list[1], (MEMBERS, LEVELS, NX, NY), MEMBERS ** -0.5, 0.75, ((0, 8), (2, 32)))
    innovation = bell_draw(key_list[2], (LEVELS, NX, NY), 1.0, 6.0, ((1, 32),), jnp.float32)
    precision_obs = jnp.clip(jnp.exp(math.log(4.0) - 1.3862944 * jax.random.uniform(key_list[3], (LEVELS, NX, NY), jnp.float32) ** shard_levels(key_list[3], (LEVELS, NX, NY), ((1, 32),), -0.2, 0.2)), 1.0, 4.0)
    classes_x = jax.random.randint(key_list[4], (NX // BLOCK,), 0, CLASSES).astype(jnp.int32)
    classes_y = plant(jax.random.randint(key_list[5], (NY // BLOCK,), 0, CLASSES), jax.random.fold_in(key_list[5], 1), 0, CLASSES - 1).astype(jnp.int32)
    tables_x = draw_tables_x(jax.random.fold_in(key_list[8], 71), 0)
    tables_y = draw_tables_y(jax.random.fold_in(key_list[8], 71), 0)
    return dict(control=control, ensemble=ensemble, innovation=innovation, precision_obs=precision_obs, classes_x=classes_x, classes_y=classes_y, tables_x=tables_x, tables_y=tables_y)


def band_apply(values, tables, classes):
    tile_size = tables.shape[-1]
    band_count = tables.shape[1]
    margin = (band_count - 1) // 2
    leading = values.shape[:-1]
    tile_count = values.shape[-1] // tile_size
    blocks = values.reshape(leading + (tile_count, tile_size)).astype(jnp.float32)
    padded = jnp.pad(blocks, [(0, 0)] * len(leading) + [(margin, margin), (0, 0)])
    windows = jnp.stack([padded[..., slot_index:slot_index + tile_count, :] for slot_index in range(band_count)], axis=-2)
    chosen = tables[classes].astype(jnp.float32)
    result = jnp.einsum("...bki,bkij->...bj", windows, chosen)
    return result.reshape(leading + (tile_count * tile_size,))


def band_adjoint(values, tables, classes):
    tile_size = tables.shape[-1]
    band_count = tables.shape[1]
    margin = (band_count - 1) // 2
    leading = values.shape[:-1]
    tile_count = values.shape[-1] // tile_size
    blocks = values.reshape(leading + (tile_count, tile_size)).astype(jnp.float32)
    chosen = tables[classes].astype(jnp.float32)
    pieces = jnp.einsum("...bj,bkij->...bki", blocks, chosen)
    padded = jnp.pad(pieces, [(0, 0)] * len(leading) + [(margin, margin), (0, 0), (0, 0)])
    result = jnp.zeros(leading + (tile_count, tile_size), jnp.float32)
    for slot_index in range(band_count):
        begin = 2 * margin - slot_index
        result = result + padded[..., begin:begin + tile_count, slot_index, :]
    return result.reshape(leading + (tile_count * tile_size,))


def reference(control, ensemble, innovation, precision_obs, classes_x, classes_y, tables_x, tables_y):
    def forward(summed, member):
        control_m, ensemble_m = member
        smooth_x = band_apply(control_m, tables_x, classes_x).astype(jnp.bfloat16)
        turned = jnp.swapaxes(smooth_x, 1, 2)
        smooth_y = band_apply(turned, tables_y, classes_y)
        return summed + ensemble_m.astype(jnp.float32) * smooth_y, None

    start_sum = jnp.zeros(innovation.shape, jnp.float32)
    increment, unused = lax.scan(forward, start_sum, (control, ensemble))
    weighted_res = precision_obs * (increment - innovation)

    def backward(member):
        control_m, ensemble_m = member
        member_force = (ensemble_m.astype(jnp.float32) * weighted_res).astype(jnp.bfloat16)
        back_y = band_adjoint(member_force, tables_y, classes_y).astype(jnp.bfloat16)
        turned = jnp.swapaxes(back_y, 1, 2)
        back_x = band_adjoint(turned, tables_x, classes_x)
        return (control_m.astype(jnp.float32) + back_x).astype(jnp.bfloat16)

    gradient = lax.map(backward, (control, ensemble))
    return increment, gradient
```

```python
import jax
import jax.numpy as jnp
from jax import lax
from jax.experimental import pallas as pl
from jax.experimental.pallas import tpu as pltpu
from jax.sharding import PartitionSpec as P

MESH = pl.DeviceIdType.MESH
F32 = jnp.float32
BF16 = jnp.bfloat16
NT = (((1,), (1,)), ((), ()))
TN = (((0,), (0,)), ((), ()))

SPACE = 32
MEM = 8
XS = 4
M = 7
LEVELS = 8
CHUNKS = 2
LC = LEVELS // CHUNKS
ROWS = 32
COLS = 8
NX = 256
NY = 1024
B = 128
NB = NY // B
LANES = M * LC * ROWS


def swap_groups(tiles):
    a, b, c, d = tiles
    axis = a.ndim - 1
    lane = lax.broadcasted_iota(jnp.int32, a.shape, axis)
    low = lane < 64
    even = lax.rem(lane, 64) < 32

    def far(p, q):
        return jnp.where(low, p, pltpu.roll(q, 64, axis)), jnp.where(low, pltpu.roll(p, 64, axis), q)

    def near(p, q):
        return jnp.where(even, p, pltpu.roll(q, 32, axis)), jnp.where(even, pltpu.roll(p, 96, axis), q)

    a, c = far(a, c)
    b, d = far(b, d)
    a, b = near(a, b)
    c, d = near(c, d)
    return a, b, c, d


def kernel(
    classes_x, classes_y, control, ensemble, innovation, precision, tables_x, tables_y,
    increment, gradient,
    ctl, ens, inn, prec, tx, ty, wxt, wy, send1, recv1, send2, recv2, field, part, rs_recv, zsend, zrecv,
    wres, inc, grad,
    in_sem, out_sem, s1_sem, r1_sem, s2_sem, r2_sem, xs_sem, xr_sem, zs_sem, zr_sem, ws_sem, wr_sem,
):
    me = lax.axis_index("space")
    mem = lax.axis_index("mem")
    my_x = lax.rem(mem, XS)
    my_hi = mem // XS
    base = my_hi * XS

    def lv(c):
        return pl.ds(c * LC, LC)

    loads = {
        "ctl0": pltpu.make_async_copy(control.at[:, lv(0)], ctl.at[:, lv(0)], in_sem.at[0]),
        "tx": pltpu.make_async_copy(tables_x, tx, in_sem.at[1]),
        "ctl1": pltpu.make_async_copy(control.at[:, lv(1)], ctl.at[:, lv(1)], in_sem.at[2]),
        "ty": pltpu.make_async_copy(tables_y, ty, in_sem.at[3]),
        "ens": pltpu.make_async_copy(ensemble, ens, in_sem.at[4]),
        "inn0": pltpu.make_async_copy(innovation.at[my_x], inn.at[0], in_sem.at[5]),
        "inn1": pltpu.make_async_copy(innovation.at[LC + my_x], inn.at[1], in_sem.at[6]),
        "prec0": pltpu.make_async_copy(precision.at[my_x], prec.at[0], in_sem.at[7]),
        "prec1": pltpu.make_async_copy(precision.at[LC + my_x], prec.at[1], in_sem.at[8]),
    }
    for copy in loads.values():
        copy.start()

    barrier = pltpu.get_barrier_semaphore()

    @pl.loop(1, SPACE)
    def _(k):
        pl.semaphore_signal(barrier, inc=1, device_id={"space": lax.rem(me + k, SPACE)}, device_id_type=MESH)

    def x_peer(k):
        return lax.rem(my_x + k, XS)

    for k in range(1, XS):
        pl.semaphore_signal(barrier, inc=1, device_id={"mem": base + x_peer(k)}, device_id_type=MESH)
    other_half = lax.rem(mem + XS, MEM)
    pl.semaphore_signal(barrier, inc=1, device_id={"mem": other_half}, device_id_type=MESH)

    loads["tx"].wait()
    for b in range(2):
        for j in range(2):
            block = tx[classes_x[b], j - b + 2]
            wxt[b * B : (b + 1) * B, j * B : (j + 1) * B] = block.astype(F32).T.astype(BF16)

    def x_filter(c):
        for m in range(M):
            rows = ctl[m, c * LC : (c + 1) * LC].reshape(LC * ROWS, NX)
            out = lax.dot_general(wxt[...], rows, NT, preferred_element_type=F32)
            send1[c, :, :, m * B : (m + 1) * B] = out.reshape(SPACE, COLS, B).astype(BF16)

    def space_copy(send, recv, s_sem, r_sem, c, d):
        return pltpu.make_async_remote_copy(
            src_ref=send.at[c, d], dst_ref=recv.at[c, me], send_sem=s_sem.at[c], recv_sem=r_sem.at[c],
            device_id={"space": d}, device_id_type=MESH,
        )

    def all_wait(send, recv, sem, c):
        pltpu.make_async_copy(send.at[c, pl.ds(0, SPACE - 1)], recv.at[c, pl.ds(0, SPACE - 1)], sem.at[c]).wait()

    def start_all(send, recv, s_sem, r_sem, c):
        @pl.loop(1, SPACE)
        def _(k):
            space_copy(send, recv, s_sem, r_sem, c, lax.rem(me + k, SPACE)).start()

        recv[c, me] = send[c, me]

    loads["ctl0"].wait()
    x_filter(0)
    pl.semaphore_wait(barrier, SPACE + XS - 1)
    start_all(send1, recv1, s1_sem, r1_sem, 0)
    loads["ctl1"].wait()
    x_filter(1)

    loads["ty"].wait()
    for b in range(NB):
        for j in range(NB):
            if abs(j - b) <= 2:
                wy[j * B : (j + 1) * B, b * B : (b + 1) * B] = ty[classes_y[b], j - b + 2]
            elif abs(j - b) == 3:
                wy[j * B : (j + 1) * B, b * B : (b + 1) * B] = jnp.zeros((B, B), BF16)

    def band(s):
        return max(0, 2 * s - 2) * B, min(NB, 2 * s + 4) * B

    loads["ens"].wait()
    for name in ("inn0", "inn1", "prec0", "prec1"):
        loads[name].wait()
    all_wait(send1, recv1, s1_sem, 0)
    start_all(send1, recv1, s1_sem, r1_sem, 1)

    def to_fields(c):
        for m in range(M):
            block = recv1[c, :, :, m * B : (m + 1) * B].astype(F32).reshape(NB, 4, COLS, B)
            out = swap_groups([block[:, j] for j in range(4)])
            for b in range(NB):
                tile = jnp.concatenate([out[i][b] for i in range(4)], axis=0)
                field[m * 32 : (m + 1) * 32, b * B : (b + 1) * B] = tile.astype(BF16)

    def members(c, m, lo, hi):
        return ens[m, c * LC : (c + 1) * LC, :, lo:hi].astype(F32).reshape(LC * COLS, hi - lo)

    def forward(c):
        to_fields(c)
        for s in range(NB // 2):
            lo, hi = band(s)
            left, right = 2 * s * B, 2 * (s + 1) * B
            out = jnp.dot(field[:, lo:hi], wy[lo:hi, left:right], preferred_element_type=F32)
            total = jnp.zeros((LC * COLS, 2 * B), F32)
            for m in range(M):
                total = total + members(c, m, left, right) * out[m * 32 : (m + 1) * 32]
            part[c, :, :, left:right] = total.reshape(LC, COLS, 2 * B)

    def reduce(c):
        copies = []
        for k in range(1, XS):
            p = x_peer(k)
            copies.append(pltpu.make_async_remote_copy(
                src_ref=part.at[c, p], dst_ref=rs_recv.at[c, my_x], send_sem=xs_sem.at[c], recv_sem=xr_sem.at[c],
                device_id={"mem": base + p}, device_id_type=MESH,
            ))
        for copy in copies:
            copy.start()
        rs_recv[c, my_x] = part[c, my_x]
        pltpu.make_async_copy(part.at[c, pl.ds(0, XS - 1)], rs_recv.at[c, pl.ds(0, XS - 1)], xr_sem.at[c]).wait()
        zsend[c] = (rs_recv[c, 0] + rs_recv[c, 1]) + (rs_recv[c, 2] + rs_recv[c, 3])
        copy = pltpu.make_async_remote_copy(
            src_ref=zsend.at[c], dst_ref=zrecv.at[c], send_sem=zs_sem.at[c], recv_sem=zr_sem.at[c],
            device_id={"mem": other_half}, device_id_type=MESH,
        )
        copy.start()
        pltpu.make_async_copy(part.at[c, pl.ds(0, XS - 1)], rs_recv.at[c, pl.ds(0, XS - 1)], xs_sem.at[c]).wait()
        copy.wait()
        total = zsend[c] + zrecv[c]

        @pl.when(my_hi == c)
        def _():
            inc[0] = total

        wres[c, my_x] = (prec[c] * (total - inn[c])).astype(BF16)
        copies = []
        for k in range(1, XS):
            copies.append(pltpu.make_async_remote_copy(
                src_ref=wres.at[c, my_x], dst_ref=wres.at[c, my_x], send_sem=ws_sem.at[c], recv_sem=wr_sem.at[c],
                device_id={"mem": base + x_peer(k)}, device_id_type=MESH,
            ))
        for copy in copies:
            copy.start()
        for sem in (ws_sem, wr_sem):
            pltpu.make_async_copy(wres.at[c, pl.ds(0, XS - 1)], wres.at[c, pl.ds(0, XS - 1)], sem.at[c]).wait()

    def backward(c):
        weight = wres[c].astype(F32).reshape(LC * COLS, NY)
        for m in range(M):
            field[m * 32 : (m + 1) * 32] = (members(c, m, 0, NY) * weight).astype(BF16)
        for s in range(NB // 2):
            lo, hi = band(s)
            out = lax.dot_general(
                field[:, lo:hi], wy[2 * s * B : 2 * (s + 1) * B, lo:hi], NT, preferred_element_type=F32
            )
            for half in range(2):
                for m in range(M):
                    rows = out[m * 32 : (m + 1) * 32, half * B : (half + 1) * B].reshape(LC, COLS, B)
                    tiles = swap_groups([rows[i] for i in range(4)])
                    for j in range(4):
                        send2[c, 8 * s + 4 * half + j, :, m * B : (m + 1) * B] = tiles[j].astype(BF16)

    def out_copy(c):
        return pltpu.make_async_copy(grad.at[:, lv(c)], gradient.at[:, lv(c)], out_sem.at[c])

    def finish(c):
        for m in range(M):
            cols = recv2[c, :, :, m * B : (m + 1) * B].astype(F32).reshape(NX, B).astype(BF16)
            out = lax.dot_general(cols, wxt[...], TN, preferred_element_type=F32)
            base_rows = ctl[m, c * LC : (c + 1) * LC].astype(F32)
            grad[m, c * LC : (c + 1) * LC] = (base_rows + out.reshape(LC, ROWS, NX)).astype(BF16)
        out_copy(c).start()

    all_wait(send1, recv1, r1_sem, 0)
    forward(0)
    reduce(0)
    backward(0)
    all_wait(send1, recv1, s1_sem, 1)
    start_all(send2, recv2, s2_sem, r2_sem, 0)
    all_wait(send1, recv1, r1_sem, 1)
    forward(1)
    reduce(1)
    inc_copy = pltpu.make_async_copy(inc, increment, out_sem.at[2])
    inc_copy.start()
    backward(1)
    all_wait(send2, recv2, s2_sem, 0)
    start_all(send2, recv2, s2_sem, r2_sem, 1)
    all_wait(send2, recv2, r2_sem, 0)
    finish(0)
    all_wait(send2, recv2, s2_sem, 1)
    all_wait(send2, recv2, r2_sem, 1)
    finish(1)
    inc_copy.wait()
    out_copy(0).wait()
    out_copy(1).wait()


def per_device(control, ensemble, innovation, precision_obs, classes_x, classes_y, tables_x, tables_y):
    any_space = pl.BlockSpec(memory_space=pl.ANY)
    smem = pl.BlockSpec(memory_space=pltpu.SMEM)
    dma = pltpu.SemaphoreType.DMA
    message = pltpu.VMEM((CHUNKS, SPACE, COLS, LANES), BF16)
    return pl.pallas_call(
        kernel,
        out_shape=(
            jax.ShapeDtypeStruct((1, COLS, NY), F32),
            jax.ShapeDtypeStruct((M, LEVELS, ROWS, NX), BF16),
        ),
        in_specs=[smem, smem] + [any_space] * 6,
        out_specs=(any_space, any_space),
        scratch_shapes=[
            pltpu.VMEM((M, LEVELS, ROWS, NX), BF16),
            pltpu.VMEM((M, LEVELS, COLS, NY), BF16),
            pltpu.VMEM((CHUNKS, COLS, NY), F32),
            pltpu.VMEM((CHUNKS, COLS, NY), F32),
            pltpu.VMEM(tables_x.shape, BF16),
            pltpu.VMEM(tables_y.shape, BF16),
            pltpu.VMEM((NX, NX), BF16),
            pltpu.VMEM((NY, NY), BF16),
            message, message, message, message,
            pltpu.VMEM((M * LC * COLS, NY), BF16),
            pltpu.VMEM((CHUNKS, LC, COLS, NY), F32),
            pltpu.VMEM((CHUNKS, XS, COLS, NY), F32),
            pltpu.VMEM((CHUNKS, COLS, NY), F32),
            pltpu.VMEM((CHUNKS, COLS, NY), F32),
            pltpu.VMEM((CHUNKS, XS, COLS, NY), BF16),
            pltpu.VMEM((1, COLS, NY), F32),
            pltpu.VMEM((M, LEVELS, ROWS, NX), BF16),
            dma((9,)), dma((3,)),
        ] + [dma((CHUNKS,))] * 10,
        compiler_params=pltpu.CompilerParams(
            collective_id=0, has_side_effects=True, vmem_limit_bytes=63 << 20
        ),
        name="hybrid_envar",
    )(classes_x, classes_y, control, ensemble, innovation, precision_obs, tables_x, tables_y)


def solution(mesh):
    in_specs = (
        P("mem", None, "space", None),
        P("mem", None, "space", None),
        P(None, "space", None),
        P(None, "space", None),
        P(),
        P(),
        P(),
        P(),
    )
    out_specs = (P("mem", "space", None), P("mem", None, "space", None))
    return jax.shard_map(
        per_device, mesh=mesh, in_specs=in_specs, out_specs=out_specs, check_vma=False
    )
```

```python
import jax
import jax.numpy as jnp
from jax import lax
from jax.experimental import pallas as pl
from jax.experimental.pallas import tpu as pltpu
from jax.sharding import PartitionSpec as P

MESH = pl.DeviceIdType.MESH
F32 = jnp.float32
BF16 = jnp.bfloat16
NT = (((1,), (1,)), ((), ()))
TN = (((0,), (0,)), ((), ()))

SPACE = 32
LEADER = 2
MEM = 8
XS = 4
M = 7
PAIRS = M // 2
LEVELS = 8
CHUNKS = 4
BATCHES = 4
QUADS = CHUNKS // 2
ROWS = 32
COLS = 8
NX = 256
NY = 1024
B = 128
NB = NY // B
HALF = NY // 2
TILES = 2 * PAIRS + 1
SHARED = PAIRS
FIELD = M * 2 * COLS


def swap_groups(tiles):
    a, b, c, d = tiles
    axis = a.ndim - 1
    lane = lax.broadcasted_iota(jnp.int32, a.shape, axis)
    low = lane < 64
    even = lax.rem(lane, 64) < 32

    def far(p, q):
        return jnp.where(low, p, pltpu.roll(q, 64, axis)), jnp.where(low, pltpu.roll(p, 64, axis), q)

    def near(p, q):
        return jnp.where(even, p, pltpu.roll(q, 32, axis)), jnp.where(even, pltpu.roll(p, 96, axis), q)

    a, c = far(a, c)
    b, d = far(b, d)
    a, b = near(a, b)
    c, d = near(c, d)
    return a, b, c, d


def lanes(t, n=1):
    return slice(t * B, (t + n) * B)


def tiles_forward(c):
    return (0, SHARED + 1) if c % 2 == 0 else (SHARED + 1, TILES)


def tiles_backward(c):
    return (0, SHARED) if c % 2 == 0 else (SHARED, TILES)


def tile_slabs(quad, t):
    if t == SHARED:
        return slice(M - 1, M), slice(4 * quad, 4 * quad + 4)
    half, pair = (0, t) if t < SHARED else (1, t - SHARED - 1)
    first = 4 * quad + 2 * half
    return slice(2 * pair, 2 * pair + 2), slice(first, first + 2)


def kernel(
    classes_x_in, classes_y_in, control, ensemble, innovation, precision, tables_x, tables_y,
    increment, gradient,
    classes_x, classes_y, ctl, ens, inn, prec, tx, ty, wxt, wy, send1, recv1, send2, recv2, field, keep, part, rs_recv, mine, half_send, zrecv,
    total, wres, inc, grad,
    in_sem, out_sem, inc_sem, s1_sem, r1_sem, s2_sem, r2_sem, xs_sem, xr_sem, zs_sem, zr_sem, ws_sem, wr_sem, group_sem, ready_sem,
):
    me = lax.axis_index("space")
    mem = lax.axis_index("mem")
    my_x = lax.rem(mem, XS)
    my_hi = mem // XS
    base = my_hi * XS
    my_level = lax.rem(my_x, 2)
    my_half = my_x // 2
    other_half = lax.rem(mem + XS, MEM)
    across = base + lax.rem(my_x + 2, XS)

    def piece(ref, c):
        return ref.at[2 * c + my_level, :, pl.ds(pl.multiple_of(my_half * HALF, HALF), HALF)]

    loads = []

    def load(src, dst):
        loads.append(pltpu.make_async_copy(src, dst, in_sem.at[len(loads)]))
        loads[-1].start()
        return loads[-1]

    ld_classes = [load(classes_x_in, classes_x), load(classes_y_in, classes_y)]
    ld_tx = load(tables_x, tx)
    ld_ctl = [load(control.at[:, pl.ds(4 * q, 4)], ctl.at[:, pl.ds(4 * q, 4)]) for q in range(QUADS)]
    ld_ty = load(tables_y, ty)
    ld_ens = load(ensemble, ens)
    ld_obs = [load(piece(innovation, c), inn.at[c]) for c in range(CHUNKS)]
    ld_obs += [load(piece(precision, c), prec.at[c]) for c in range(CHUNKS)]

    barrier = pltpu.get_barrier_semaphore()

    @pl.loop(1, SPACE)
    def _(k):
        pl.semaphore_signal(barrier, inc=1, device_id={"space": lax.rem(me + k, SPACE)}, device_id_type=MESH)

    def x_peer(k):
        return lax.rem(my_x + k, XS)

    leads = me == LEADER
    groups = [base + x_peer(k) for k in range(1, XS)] + [other_half]

    @pl.when(leads)
    def _():
        for group in groups:
            pl.semaphore_signal(barrier, inc=1, device_id={"mem": group}, device_id_type=MESH)

    def enter():
        @pl.when(leads)
        def _():
            pl.semaphore_wait(barrier, SPACE - 1 + len(groups))
            for group in groups:
                pl.semaphore_signal(group_sem, inc=1, device_id={"mem": group}, device_id_type=MESH)

        @pl.when(jnp.logical_not(leads))
        def _():
            pl.semaphore_wait(barrier, SPACE - 1)

    def enter_groups():
        @pl.when(leads)
        def _():
            pl.semaphore_wait(group_sem, len(groups))

            @pl.loop(1, SPACE)
            def _(k):
                pl.semaphore_signal(
                    ready_sem, inc=1, device_id={"space": lax.rem(me + k, SPACE)}, device_id_type=MESH
                )

        @pl.when(jnp.logical_not(leads))
        def _():
            pl.semaphore_wait(ready_sem, 1)

    for copy in ld_classes:
        copy.wait()
    ld_tx.wait()
    for b in range(NX // B):
        for j in range(NX // B):
            block = tx[classes_x[b], j - b + 2]
            wxt[lanes(b), lanes(j)] = block.astype(F32).T.astype(BF16)

    def x_filter(c):
        for t in range(*tiles_forward(c)):
            members, levels = tile_slabs(c // 2, t)
            rows = ctl[members, levels].reshape(4 * ROWS, NX)
            out = lax.dot_general(wxt[...], rows, NT, preferred_element_type=F32)
            send1[c // 2, :, :, lanes(t)] = out.reshape(SPACE, COLS, B).astype(BF16)

    def part_of(tiles, c):
        first, last = tiles(c)
        return pl.ds(first * B, (last - first) * B)

    def space_wait(send, recv, tiles, sem, c):
        cut = (c // 2, pl.ds(0, SPACE - 1), slice(None), part_of(tiles, c))
        pltpu.make_async_copy(send.at[cut], recv.at[cut], sem.at[c]).wait()

    def space_start(send, recv, tiles, s_sem, r_sem, c):
        q, cut = c // 2, part_of(tiles, c)

        @pl.loop(1, SPACE)
        def _(k):
            d = lax.rem(me + k, SPACE)
            pltpu.make_async_remote_copy(
                src_ref=send.at[q, d, :, cut], dst_ref=recv.at[q, me, :, cut],
                send_sem=s_sem.at[c], recv_sem=r_sem.at[c],
                device_id={"space": d}, device_id_type=MESH,
            ).start()

        recv[q, me, :, cut] = send[q, me, :, cut]

    def start1(c, batch):
        q, cut = c // 2, part_of(tiles_forward, c)

        @pl.loop(1 if batch == 0 else 0, SPACE // BATCHES)
        def _(t):
            d = lax.rem(me + BATCHES * t + batch, SPACE)
            pltpu.make_async_remote_copy(
                src_ref=send1.at[q, d, :, cut], dst_ref=recv1.at[q, me, :, cut],
                send_sem=s1_sem.at[c, batch], recv_sem=r1_sem.at[c],
                device_id={"space": d}, device_id_type=MESH,
            ).start()

        if batch == 0:
            recv1[q, me, :, cut] = send1[q, me, :, cut]

    def sent1(c, batch):
        n = SPACE // BATCHES - (batch == 0)
        cut = (c // 2, pl.ds(0, n), slice(None), part_of(tiles_forward, c))
        pltpu.make_async_copy(send1.at[cut], recv1.at[cut], s1_sem.at[c, batch]).wait()

    def follow1(c, batch):
        sent1(c - 1, batch)
        start1(c, batch)

    def got1(c):
        space_wait(send1, recv1, tiles_forward, r1_sem, c)

    def start2(c):
        space_start(send2, recv2, tiles_backward, s2_sem, r2_sem, c)

    def sent2(c):
        space_wait(send2, recv2, tiles_backward, s2_sem, c)

    def got2(c):
        space_wait(send2, recv2, tiles_backward, r2_sem, c)

    def band(s):
        return max(0, 2 * s - 2) * B, min(NB, 2 * s + 4) * B

    def to_fields(c):
        q = c // 2
        for t in range(*tiles_forward(c)):
            block = recv1[q, :, :, lanes(t)].astype(F32).reshape(NB, 4, COLS, B)
            out = swap_groups([block[:, j] for j in range(4)])
            for b in range(NB):
                tile = jnp.concatenate([out[i][b] for i in range(4)], axis=0).astype(BF16)
                if t == SHARED:
                    field[c, 2 * PAIRS * 16 :, lanes(b)] = tile[:16]
                    field[c + 1, 2 * PAIRS * 16 :, lanes(b)] = tile[16:]
                else:
                    row = (t if t < SHARED else t - SHARED - 1) * 32
                    field[c, row : row + 32, lanes(b)] = tile

    def member(c, m, cols):
        return ens[m, 2 * c : 2 * c + 2, :, cols].astype(F32).reshape(2 * COLS, -1)

    def forward(c):
        to_fields(c)
        for s in range(NB // 2):
            lo, hi = band(s)
            cols = lanes(2 * s, 2)
            out = jnp.dot(field[c, :, lo:hi], wy[lo:hi, cols], preferred_element_type=F32)
            acc = member(c, 0, cols) * out[:16]
            for m in range(1, M):
                acc = acc + member(c, m, cols) * out[16 * m : 16 * (m + 1)]
            for level in range(2):
                part[c, 2 * (s // 2) + level, :, lanes(2 * (s % 2), 2)] = acc[COLS * level : COLS * (level + 1)]
        for k in range(1, XS):
            p = x_peer(k)
            pltpu.make_async_remote_copy(
                src_ref=part.at[c, p], dst_ref=rs_recv.at[c, my_x], send_sem=xs_sem.at[c], recv_sem=xr_sem.at[c],
                device_id={"mem": base + p}, device_id_type=MESH,
            ).start()
        rs_recv[c, my_x] = part[c, my_x]

    def peers_wait(ref, sem, c):
        cut = (c, pl.ds(0, XS - 1))
        pltpu.make_async_copy(ref.at[cut], ref.at[cut], sem.at[c]).wait()

    def half_copy(c):
        return pltpu.make_async_remote_copy(
            src_ref=half_send.at[c], dst_ref=zrecv.at[c], send_sem=zs_sem.at[c], recv_sem=zr_sem.at[c],
            device_id={"mem": other_half}, device_id_type=MESH,
        )

    def sum_x(c):
        peers_wait(rs_recv, xr_sem, c)
        mine[c] = (rs_recv[c, 0] + rs_recv[c, 1]) + (rs_recv[c, 2] + rs_recv[c, 3])
        half_send[c] = mine[c].astype(BF16)
        half_copy(c).start()

    def weigh(c):
        half_copy(c).wait_recv()
        total[c] = mine[c] + zrecv[c].astype(F32)
        wres[c, my_x] = (prec[c] * (total[c] - inn[c])).astype(BF16)
        for k in range(1, XS):
            pltpu.make_async_remote_copy(
                src_ref=wres.at[c, my_x], dst_ref=wres.at[c, my_x], send_sem=ws_sem.at[c], recv_sem=wr_sem.at[c],
                device_id={"mem": base + x_peer(k)}, device_id_type=MESH,
            ).start()

    def backward(c):
        q, odd = c // 2, c % 2
        peers_wait(wres, wr_sem, c)
        weight = jnp.concatenate(
            [
                jnp.concatenate([wres[c, level].astype(F32), wres[c, 2 + level].astype(F32)], axis=1)
                for level in range(2)
            ],
            axis=0,
        )
        for m in range(M):
            field[c, 16 * m : 16 * (m + 1)] = (member(c, m, slice(None)) * weight).astype(BF16)
        for s in range(NB // 2):
            lo, hi = band(s)
            out = lax.dot_general(field[c, :, lo:hi], wy[lanes(2 * s, 2), lo:hi], NT, preferred_element_type=F32)
            for b in (2 * s, 2 * s + 1):
                cols = lanes(b - 2 * s)
                groups = [
                    (pair + odd * (SHARED + 1), out[32 * pair : 32 * (pair + 1), cols]) for pair in range(PAIRS)
                ]
                last = out[32 * PAIRS :, cols]
                if odd:
                    groups.append((SHARED, jnp.concatenate([keep[:, lanes(b)], last], axis=0)))
                else:
                    keep[:, lanes(b)] = last
                for t, rows in groups:
                    rows = rows.reshape(4, COLS, B)
                    swapped = swap_groups([rows[i] for i in range(4)])
                    for j in range(4):
                        send2[q, 4 * b + j, :, lanes(t)] = swapped[j].astype(BF16)
        start2(c)

    def out_copies(c):
        pairs = (slice(0, 2 * PAIRS), slice(2 * c, 2 * c + 2))
        copies = [pltpu.make_async_copy(grad.at[pairs], gradient.at[pairs], out_sem.at[c])]
        if c % 2:
            last = (slice(M - 1, M), slice(2 * c - 2, 2 * c + 2))
            copies.append(pltpu.make_async_copy(grad.at[last], gradient.at[last], out_sem.at[CHUNKS + c // 2]))
        return copies

    def finish(c):
        got2(c)
        for t in range(*tiles_backward(c)):
            slabs = tile_slabs(c // 2, t)
            cols = recv2[c // 2, :, :, lanes(t)].astype(F32).reshape(NX, B).astype(BF16)
            out = lax.dot_general(cols, wxt[...], TN, preferred_element_type=F32)
            old = ctl[slabs]
            grad[slabs] = (old.astype(F32) + out.reshape(old.shape)).astype(BF16)
        for copy in out_copies(c):
            copy.start()

    ld_ctl[0].wait()
    x_filter(0)
    enter()
    for batch in range(BATCHES):
        start1(0, batch)
    x_filter(1)
    ld_ctl[1].wait()
    follow1(1, 0)
    x_filter(2)
    follow1(1, 1)
    x_filter(3)
    enter_groups()

    ld_ty.wait()
    for b in range(NB):
        for j in range(NB):
            if abs(j - b) <= 2:
                wy[lanes(j), lanes(b)] = ty[classes_y[b], j - b + 2]
            elif abs(j - b) == 3:
                wy[lanes(j), lanes(b)] = jnp.zeros((B, B), BF16)
    ld_ens.wait()
    for copy in ld_obs:
        copy.wait()

    follow1(1, 2)
    follow1(1, 3)
    got1(0)
    forward(0)
    for batch in range(BATCHES):
        follow1(2, batch)
    got1(1)
    forward(1)
    sum_x(0)
    for batch in range(BATCHES):
        follow1(3, batch)
    got1(2)
    forward(2)
    sum_x(1)
    weigh(0)
    got1(3)
    forward(3)
    sum_x(2)
    backward(0)
    weigh(1)
    sum_x(3)
    backward(1)
    weigh(2)
    backward(2)
    weigh(3)

    kept = pl.ds(pl.multiple_of(my_half * HALF, HALF), HALF)
    inc[0, :, kept] = total[2 * my_hi + my_half]
    given = pltpu.make_async_remote_copy(
        src_ref=total.at[2 * my_hi + 1 - my_half], dst_ref=inc.at[0, :, kept],
        send_sem=inc_sem.at[0], recv_sem=inc_sem.at[1], device_id={"mem": across}, device_id_type=MESH,
    )
    given.start()
    backward(3)
    finish(0)
    finish(1)
    given.wait()
    inc_copy = pltpu.make_async_copy(inc, increment, out_sem.at[CHUNKS + QUADS])
    inc_copy.start()
    finish(2)
    for c in range(CHUNKS):
        peers_wait(rs_recv, xs_sem, c)
        half_copy(c).wait_send()
        peers_wait(wres, ws_sem, c)
        sent2(c)
    for batch in range(BATCHES):
        sent1(CHUNKS - 1, batch)
    finish(3)
    inc_copy.wait()
    for c in range(CHUNKS):
        for copy in out_copies(c):
            copy.wait()


def per_device(control, ensemble, innovation, precision_obs, classes_x, classes_y, tables_x, tables_y):
    any_space = pl.BlockSpec(memory_space=pl.ANY)
    dma = pltpu.SemaphoreType.DMA
    message = pltpu.VMEM((QUADS, SPACE, COLS, TILES * B), BF16)
    sums = pltpu.VMEM((CHUNKS, XS, COLS, HALF), F32)
    piece = pltpu.VMEM((CHUNKS, COLS, HALF), F32)
    return pl.pallas_call(
        kernel,
        out_shape=(
            jax.ShapeDtypeStruct((1, COLS, NY), F32),
            jax.ShapeDtypeStruct((M, LEVELS, ROWS, NX), BF16),
        ),
        in_specs=[any_space] * 8,
        out_specs=(any_space, any_space),
        scratch_shapes=[
            pltpu.SMEM(classes_x.shape, jnp.int32),
            pltpu.SMEM(classes_y.shape, jnp.int32),
            pltpu.VMEM((M, LEVELS, ROWS, NX), BF16),
            pltpu.VMEM((M, LEVELS, COLS, NY), BF16),
            piece,
            piece,
            pltpu.VMEM(tables_x.shape, BF16),
            pltpu.VMEM(tables_y.shape, BF16),
            pltpu.VMEM((NX, NX), BF16),
            pltpu.VMEM((NY, NY), BF16),
            message,
            message,
            message,
            message,
            pltpu.VMEM((CHUNKS, FIELD, NY), BF16),
            pltpu.VMEM((2 * COLS, NY), F32),
            sums,
            sums,
            piece,
            pltpu.VMEM((CHUNKS, COLS, HALF), BF16),
            pltpu.VMEM((CHUNKS, COLS, HALF), BF16),
            piece,
            pltpu.VMEM((CHUNKS, XS, COLS, HALF), BF16),
            pltpu.VMEM((1, COLS, NY), F32),
            pltpu.VMEM((M, LEVELS, ROWS, NX), BF16),
            dma((7 + 2 * CHUNKS,)),
            dma((CHUNKS + QUADS + 1,)),
            dma((2,)),
        ]
        + [dma((CHUNKS, BATCHES))]
        + [dma((CHUNKS,))] * 9
        + [pltpu.SemaphoreType.REGULAR] * 2,
        compiler_params=pltpu.CompilerParams(
            collective_id=0, has_side_effects=True, vmem_limit_bytes=63 << 20
        ),
        name="hybrid_envar",
    )(classes_x, classes_y, control, ensemble, innovation, precision_obs, tables_x, tables_y)


def solution(mesh):
    in_specs = (
        P("mem", None, "space", None),
        P("mem", None, "space", None),
        P(None, "space", None),
        P(None, "space", None),
        P(),
        P(),
        P(),
        P(),
    )
    out_specs = (P("mem", "space", None), P("mem", None, "space", None))
    return jax.shard_map(
        per_device, mesh=mesh, in_specs=in_specs, out_specs=out_specs, check_vma=False
    )
```

```python
import jax
import jax.numpy as jnp
from jax import lax
from jax.experimental import pallas as pl
from jax.experimental.pallas import tpu as pltpu
from jax.sharding import PartitionSpec as P

MESH = pl.DeviceIdType.MESH
F32 = jnp.float32
BF16 = jnp.bfloat16
NT = (((1,), (1,)), ((), ()))
TN = (((0,), (0,)), ((), ()))

SPACE = 32
LEADER = 2
MEM = 8
XS = 4
M = 7
PAIRS = M // 2
LEVELS = 8
CHUNKS = 4
BATCHES = 4
QUADS = CHUNKS // 2
ROWS = 32
COLS = 8
NX = 256
NY = 1024
B = 128
NB = NY // B
HALF = NY // 2
TILES = 2 * PAIRS + 1
SHARED = PAIRS
FIELD = M * 2 * COLS


def swap_groups(tiles):
    a, b, c, d = tiles
    axis = a.ndim - 1
    lane = lax.broadcasted_iota(jnp.int32, a.shape, axis)
    low = lane < 64
    even = lax.rem(lane, 64) < 32

    def far(p, q):
        return jnp.where(low, p, pltpu.roll(q, 64, axis)), jnp.where(low, pltpu.roll(p, 64, axis), q)

    def near(p, q):
        return jnp.where(even, p, pltpu.roll(q, 32, axis)), jnp.where(even, pltpu.roll(p, 96, axis), q)

    a, c = far(a, c)
    b, d = far(b, d)
    a, b = near(a, b)
    c, d = near(c, d)
    return a, b, c, d


def lanes(t, n=1):
    return slice(t * B, (t + n) * B)


def tiles_forward(c):
    return (0, SHARED + 1) if c % 2 == 0 else (SHARED + 1, TILES)


def tiles_backward(c):
    return (0, SHARED) if c % 2 == 0 else (SHARED, TILES)


def tile_slabs(quad, t):
    if t == SHARED:
        return slice(M - 1, M), slice(4 * quad, 4 * quad + 4)
    half, pair = (0, t) if t < SHARED else (1, t - SHARED - 1)
    first = 4 * quad + 2 * half
    return slice(2 * pair, 2 * pair + 2), slice(first, first + 2)


def kernel(
    classes_x_in, classes_y_in, control, ensemble, innovation, precision, tables_x, tables_y,
    increment, gradient,
    classes_x, classes_y, ctl, ens, inn, prec, tx, ty, wxt, wy, send1, recv1, send2, recv2, field, keep, part, rs_recv, mine, half_send, zrecv,
    total, wres, inc, grad,
    in_sem, out_sem, inc_sem, s1_sem, r1_sem, s2_sem, r2_sem, xs_sem, xr_sem, zs_sem, zr_sem, ws_sem, wr_sem, group_sem, ready_sem,
):
    me = lax.axis_index("space")
    mem = lax.axis_index("mem")
    my_x = lax.rem(mem, XS)
    my_hi = mem // XS
    base = my_hi * XS
    my_level = lax.rem(my_x, 2)
    my_half = my_x // 2
    other_half = lax.rem(mem + XS, MEM)
    across = base + lax.rem(my_x + 2, XS)

    def piece(ref, c):
        return ref.at[2 * c + my_level, :, pl.ds(pl.multiple_of(my_half * HALF, HALF), HALF)]

    loads = []

    def load(src, dst):
        loads.append(pltpu.make_async_copy(src, dst, in_sem.at[len(loads)]))
        return loads[-1]

    ld_classes = [load(classes_x_in, classes_x), load(classes_y_in, classes_y)]
    ld_tx = load(tables_x, tx)
    ld_ctl = [load(control.at[:, pl.ds(4 * q, 4)], ctl.at[:, pl.ds(4 * q, 4)]) for q in range(QUADS)]
    ld_ty = load(tables_y, ty)
    ld_ens = load(ensemble, ens)
    ld_obs = [load(piece(innovation, c), inn.at[c]) for c in range(CHUNKS)]
    ld_obs += [load(piece(precision, c), prec.at[c]) for c in range(CHUNKS)]

    urgent = ld_classes + [ld_tx, ld_ctl[0]]
    for copy in urgent:
        copy.start()

    barrier = pltpu.get_barrier_semaphore()

    @pl.loop(1, SPACE)
    def _(k):
        pl.semaphore_signal(barrier, inc=1, device_id={"space": lax.rem(me + k, SPACE)}, device_id_type=MESH)

    def x_peer(k):
        return lax.rem(my_x + k, XS)

    leads = me == LEADER
    groups = [base + x_peer(k) for k in range(1, XS)] + [other_half]

    @pl.when(leads)
    def _():
        for group in groups:
            pl.semaphore_signal(barrier, inc=1, device_id={"mem": group}, device_id_type=MESH)

    def enter():
        @pl.when(leads)
        def _():
            pl.semaphore_wait(barrier, SPACE - 1 + len(groups))
            for group in groups:
                pl.semaphore_signal(group_sem, inc=1, device_id={"mem": group}, device_id_type=MESH)

        @pl.when(jnp.logical_not(leads))
        def _():
            pl.semaphore_wait(barrier, SPACE - 1)

    def enter_groups():
        @pl.when(leads)
        def _():
            pl.semaphore_wait(group_sem, len(groups))

            @pl.loop(1, SPACE)
            def _(k):
                pl.semaphore_signal(
                    ready_sem, inc=1, device_id={"space": lax.rem(me + k, SPACE)}, device_id_type=MESH
                )

        @pl.when(jnp.logical_not(leads))
        def _():
            pl.semaphore_wait(ready_sem, 1)

    for copy in ld_classes:
        copy.wait()
    ld_tx.wait()
    for b in range(NX // B):
        for j in range(NX // B):
            block = tx[classes_x[b], j - b + 2]
            wxt[lanes(b), lanes(j)] = block.astype(F32).T.astype(BF16)

    def x_filter(c):
        for t in range(*tiles_forward(c)):
            members, levels = tile_slabs(c // 2, t)
            rows = ctl[members, levels].reshape(4 * ROWS, NX)
            out = lax.dot_general(wxt[...], rows, NT, preferred_element_type=F32)
            send1[c // 2, :, :, lanes(t)] = out.reshape(SPACE, COLS, B).astype(BF16)

    def part_of(tiles, c):
        first, last = tiles(c)
        return pl.ds(first * B, (last - first) * B)

    def space_wait(send, recv, tiles, sem, c):
        cut = (c // 2, pl.ds(0, SPACE - 1), slice(None), part_of(tiles, c))
        pltpu.make_async_copy(send.at[cut], recv.at[cut], sem.at[c]).wait()

    def space_start(send, recv, tiles, s_sem, r_sem, c):
        q, cut = c // 2, part_of(tiles, c)

        @pl.loop(1, SPACE)
        def _(k):
            d = lax.rem(me + k, SPACE)
            pltpu.make_async_remote_copy(
                src_ref=send.at[q, d, :, cut], dst_ref=recv.at[q, me, :, cut],
                send_sem=s_sem.at[c], recv_sem=r_sem.at[c],
                device_id={"space": d}, device_id_type=MESH,
            ).start()

        recv[q, me, :, cut] = send[q, me, :, cut]

    def start1(c, batch):
        q, cut = c // 2, part_of(tiles_forward, c)

        @pl.loop(1 if batch == 0 else 0, SPACE // BATCHES)
        def _(t):
            d = lax.rem(me + BATCHES * t + batch, SPACE)
            pltpu.make_async_remote_copy(
                src_ref=send1.at[q, d, :, cut], dst_ref=recv1.at[q, me, :, cut],
                send_sem=s1_sem.at[c, batch], recv_sem=r1_sem.at[c],
                device_id={"space": d}, device_id_type=MESH,
            ).start()

        if batch == 0:
            recv1[q, me, :, cut] = send1[q, me, :, cut]

    def sent1(c, batch):
        n = SPACE // BATCHES - (batch == 0)
        cut = (c // 2, pl.ds(0, n), slice(None), part_of(tiles_forward, c))
        pltpu.make_async_copy(send1.at[cut], recv1.at[cut], s1_sem.at[c, batch]).wait()

    def follow1(c, batch):
        sent1(c - 1, batch)
        start1(c, batch)

    def got1(c):
        space_wait(send1, recv1, tiles_forward, r1_sem, c)

    def start2(c):
        space_start(send2, recv2, tiles_backward, s2_sem, r2_sem, c)

    def sent2(c):
        space_wait(send2, recv2, tiles_backward, s2_sem, c)

    def got2(c):
        space_wait(send2, recv2, tiles_backward, r2_sem, c)

    def band(s):
        return max(0, 2 * s - 2) * B, min(NB, 2 * s + 4) * B

    def to_fields(c):
        q = c // 2
        for t in range(*tiles_forward(c)):
            block = recv1[q, :, :, lanes(t)].astype(F32).reshape(NB, 4, COLS, B)
            out = swap_groups([block[:, j] for j in range(4)])
            for b in range(NB):
                tile = jnp.concatenate([out[i][b] for i in range(4)], axis=0).astype(BF16)
                if t == SHARED:
                    field[c, 2 * PAIRS * 16 :, lanes(b)] = tile[:16]
                    field[c + 1, 2 * PAIRS * 16 :, lanes(b)] = tile[16:]
                else:
                    row = (t if t < SHARED else t - SHARED - 1) * 32
                    field[c, row : row + 32, lanes(b)] = tile

    def member(c, m, cols):
        return ens[m, 2 * c : 2 * c + 2, :, cols].astype(F32).reshape(2 * COLS, -1)

    def forward(c):
        to_fields(c)
        for s in range(NB // 2):
            lo, hi = band(s)
            cols = lanes(2 * s, 2)
            out = jnp.dot(field[c, :, lo:hi], wy[lo:hi, cols], preferred_element_type=F32)
            acc = member(c, 0, cols) * out[:16]
            for m in range(1, M):
                acc = acc + member(c, m, cols) * out[16 * m : 16 * (m + 1)]
            for level in range(2):
                part[c, 2 * (s // 2) + level, :, lanes(2 * (s % 2), 2)] = acc[COLS * level : COLS * (level + 1)]
        for k in range(1, XS):
            p = x_peer(k)
            pltpu.make_async_remote_copy(
                src_ref=part.at[c, p], dst_ref=rs_recv.at[c, my_x], send_sem=xs_sem.at[c], recv_sem=xr_sem.at[c],
                device_id={"mem": base + p}, device_id_type=MESH,
            ).start()
        rs_recv[c, my_x] = part[c, my_x]

    def peers_wait(ref, sem, c):
        cut = (c, pl.ds(0, XS - 1))
        pltpu.make_async_copy(ref.at[cut], ref.at[cut], sem.at[c]).wait()

    def half_copy(c):
        return pltpu.make_async_remote_copy(
            src_ref=half_send.at[c], dst_ref=zrecv.at[c], send_sem=zs_sem.at[c], recv_sem=zr_sem.at[c],
            device_id={"mem": other_half}, device_id_type=MESH,
        )

    def sum_x(c):
        peers_wait(rs_recv, xr_sem, c)
        mine[c] = (rs_recv[c, 0] + rs_recv[c, 1]) + (rs_recv[c, 2] + rs_recv[c, 3])
        half_send[c] = mine[c].astype(BF16)
        half_copy(c).start()

    def weigh(c):
        half_copy(c).wait_recv()
        total[c] = mine[c] + zrecv[c].astype(F32)
        wres[c, my_x] = (prec[c] * (total[c] - inn[c])).astype(BF16)
        for k in range(1, XS):
            pltpu.make_async_remote_copy(
                src_ref=wres.at[c, my_x], dst_ref=wres.at[c, my_x], send_sem=ws_sem.at[c], recv_sem=wr_sem.at[c],
                device_id={"mem": base + x_peer(k)}, device_id_type=MESH,
            ).start()

    def backward(c):
        q, odd = c // 2, c % 2
        peers_wait(wres, wr_sem, c)
        weight = jnp.concatenate(
            [
                jnp.concatenate([wres[c, level].astype(F32), wres[c, 2 + level].astype(F32)], axis=1)
                for level in range(2)
            ],
            axis=0,
        )
        for m in range(M):
            field[c, 16 * m : 16 * (m + 1)] = (member(c, m, slice(None)) * weight).astype(BF16)
        for s in range(NB // 2):
            lo, hi = band(s)
            out = lax.dot_general(field[c, :, lo:hi], wy[lanes(2 * s, 2), lo:hi], NT, preferred_element_type=F32)
            for b in (2 * s, 2 * s + 1):
                cols = lanes(b - 2 * s)
                groups = [
                    (pair + odd * (SHARED + 1), out[32 * pair : 32 * (pair + 1), cols]) for pair in range(PAIRS)
                ]
                last = out[32 * PAIRS :, cols]
                if odd:
                    groups.append((SHARED, jnp.concatenate([keep[:, lanes(b)], last], axis=0)))
                else:
                    keep[:, lanes(b)] = last
                for t, rows in groups:
                    rows = rows.reshape(4, COLS, B)
                    swapped = swap_groups([rows[i] for i in range(4)])
                    for j in range(4):
                        send2[q, 4 * b + j, :, lanes(t)] = swapped[j].astype(BF16)
        start2(c)

    def out_copies(c):
        pairs = (slice(0, 2 * PAIRS), slice(2 * c, 2 * c + 2))
        copies = [pltpu.make_async_copy(grad.at[pairs], gradient.at[pairs], out_sem.at[c])]
        if c % 2:
            last = (slice(M - 1, M), slice(2 * c - 2, 2 * c + 2))
            copies.append(pltpu.make_async_copy(grad.at[last], gradient.at[last], out_sem.at[CHUNKS + c // 2]))
        return copies

    def finish(c):
        got2(c)
        for t in range(*tiles_backward(c)):
            slabs = tile_slabs(c // 2, t)
            cols = recv2[c // 2, :, :, lanes(t)].astype(F32).reshape(NX, B).astype(BF16)
            out = lax.dot_general(cols, wxt[...], TN, preferred_element_type=F32)
            old = ctl[slabs]
            grad[slabs] = (old.astype(F32) + out.reshape(old.shape)).astype(BF16)
        for copy in out_copies(c):
            copy.start()

    ld_ctl[0].wait()
    for copy in loads:
        if all(copy is not other for other in urgent):
            copy.start()
    x_filter(0)
    enter()
    for batch in range(BATCHES):
        start1(0, batch)
    x_filter(1)
    ld_ctl[1].wait()
    follow1(1, 0)
    x_filter(2)
    follow1(1, 1)
    x_filter(3)
    enter_groups()

    ld_ty.wait()
    for b in range(NB):
        for j in range(NB):
            if abs(j - b) <= 2:
                wy[lanes(j), lanes(b)] = ty[classes_y[b], j - b + 2]
            elif abs(j - b) == 3:
                wy[lanes(j), lanes(b)] = jnp.zeros((B, B), BF16)
    ld_ens.wait()
    for copy in ld_obs:
        copy.wait()

    follow1(1, 2)
    follow1(1, 3)
    got1(0)
    forward(0)
    for batch in range(BATCHES):
        follow1(2, batch)
    got1(1)
    forward(1)
    sum_x(0)
    for batch in range(BATCHES):
        follow1(3, batch)
    got1(2)
    forward(2)
    sum_x(1)
    weigh(0)
    got1(3)
    forward(3)
    sum_x(2)
    backward(0)
    weigh(1)
    sum_x(3)
    backward(1)
    weigh(2)
    backward(2)
    weigh(3)

    kept = pl.ds(pl.multiple_of(my_half * HALF, HALF), HALF)
    inc[0, :, kept] = total[2 * my_hi + my_half]
    given = pltpu.make_async_remote_copy(
        src_ref=total.at[2 * my_hi + 1 - my_half], dst_ref=inc.at[0, :, kept],
        send_sem=inc_sem.at[0], recv_sem=inc_sem.at[1], device_id={"mem": across}, device_id_type=MESH,
    )
    given.start()
    backward(3)
    finish(0)
    finish(1)
    given.wait()
    inc_copy = pltpu.make_async_copy(inc, increment, out_sem.at[CHUNKS + QUADS])
    inc_copy.start()
    finish(2)
    for c in range(CHUNKS):
        peers_wait(rs_recv, xs_sem, c)
        half_copy(c).wait_send()
        peers_wait(wres, ws_sem, c)
        sent2(c)
    for batch in range(BATCHES):
        sent1(CHUNKS - 1, batch)
    finish(3)
    inc_copy.wait()
    for c in range(CHUNKS):
        for copy in out_copies(c):
            copy.wait()


def write_out(inc_in, grad_in, increment, gradient, inc, grad, sem):
    copies = [(inc_in, inc, increment)] + [(grad_in.at[m], grad.at[m], gradient.at[m]) for m in range(M)]
    loads = [pltpu.make_async_copy(src, via, sem.at[0, n]) for n, (src, via, _) in enumerate(copies)]
    stores = [pltpu.make_async_copy(via, dst, sem.at[1, n]) for n, (_, via, dst) in enumerate(copies)]
    for load in loads:
        load.start()
    for load, store in zip(loads, stores):
        load.wait()
        store.start()
    for store in stores:
        store.wait()


def per_device(control, ensemble, innovation, precision_obs, classes_x, classes_y, tables_x, tables_y):
    any_space = pl.BlockSpec(memory_space=pl.ANY)
    dma = pltpu.SemaphoreType.DMA
    message = pltpu.VMEM((QUADS, SPACE, COLS, TILES * B), BF16)
    sums = pltpu.VMEM((CHUNKS, XS, COLS, HALF), F32)
    piece = pltpu.VMEM((CHUNKS, COLS, HALF), F32)
    shapes = (
        jax.ShapeDtypeStruct((1, COLS, NY), F32),
        jax.ShapeDtypeStruct((M, LEVELS, ROWS, NX), BF16),
    )
    results = pl.pallas_call(
        kernel,
        out_shape=shapes,
        in_specs=[any_space] * 8,
        out_specs=(any_space, any_space),
        scratch_shapes=[
            pltpu.SMEM(classes_x.shape, jnp.int32),
            pltpu.SMEM(classes_y.shape, jnp.int32),
            pltpu.VMEM((M, LEVELS, ROWS, NX), BF16),
            pltpu.VMEM((M, LEVELS, COLS, NY), BF16),
            piece,
            piece,
            pltpu.VMEM(tables_x.shape, BF16),
            pltpu.VMEM(tables_y.shape, BF16),
            pltpu.VMEM((NX, NX), BF16),
            pltpu.VMEM((NY, NY), BF16),
            message,
            message,
            message,
            message,
            pltpu.VMEM((CHUNKS, FIELD, NY), BF16),
            pltpu.VMEM((2 * COLS, NY), F32),
            sums,
            sums,
            piece,
            pltpu.VMEM((CHUNKS, COLS, HALF), BF16),
            pltpu.VMEM((CHUNKS, COLS, HALF), BF16),
            piece,
            pltpu.VMEM((CHUNKS, XS, COLS, HALF), BF16),
            pltpu.VMEM((1, COLS, NY), F32),
            pltpu.VMEM((M, LEVELS, ROWS, NX), BF16),
            dma((7 + 2 * CHUNKS,)),
            dma((CHUNKS + QUADS + 1,)),
            dma((2,)),
        ]
        + [dma((CHUNKS, BATCHES))]
        + [dma((CHUNKS,))] * 9
        + [pltpu.SemaphoreType.REGULAR] * 2,
        compiler_params=pltpu.CompilerParams(
            collective_id=0, has_side_effects=True, vmem_limit_bytes=63 << 20
        ),
        name="hybrid_envar",
    )(classes_x, classes_y, control, ensemble, innovation, precision_obs, tables_x, tables_y)
    return pl.pallas_call(
        write_out,
        out_shape=shapes,
        in_specs=[any_space] * 2,
        out_specs=(any_space,) * 2,
        scratch_shapes=[pltpu.VMEM(shape.shape, shape.dtype) for shape in shapes] + [dma((2, M + 1))],
        compiler_params=pltpu.CompilerParams(vmem_limit_bytes=63 << 20),
        name="write_out",
    )(*results)


def solution(mesh):
    in_specs = (
        P("mem", None, "space", None),
        P("mem", None, "space", None),
        P(None, "space", None),
        P(None, "space", None),
        P(),
        P(),
        P(),
        P(),
    )
    out_specs = (P("mem", "space", None), P("mem", None, "space", None))
    return jax.shard_map(
        per_device, mesh=mesh, in_specs=in_specs, out_specs=out_specs, check_vma=False
    )
```

```python
import jax
import jax.numpy as jnp
from jax import lax
from jax.experimental import pallas as pl
from jax.experimental.pallas import tpu as pltpu
from jax.sharding import PartitionSpec as P

MESH = pl.DeviceIdType.MESH
F32 = jnp.float32
BF16 = jnp.bfloat16
NT = (((1,), (1,)), ((), ()))
TN = (((0,), (0,)), ((), ()))

SPACE = 32
LEADER = 2
MEM = 8
XS = 4
M = 7
PAIRS = M // 2
LEVELS = 8
CLASSES = 8
CHUNKS = 4
BATCHES = 4
QUADS = CHUNKS // 2
ROWS = 32
COLS = 8
NX = 256
NY = 1024
B = 128
NB = NY // B
HALF = NY // 2
TILES = 2 * PAIRS + 1
SHARED = PAIRS
FIELD = M * 2 * COLS


def swap_groups(tiles):
    a, b, c, d = tiles
    axis = a.ndim - 1
    lane = lax.broadcasted_iota(jnp.int32, a.shape, axis)
    low = lane < 64
    even = lax.rem(lane, 64) < 32

    def far(p, q):
        return jnp.where(low, p, pltpu.roll(q, 64, axis)), jnp.where(low, pltpu.roll(p, 64, axis), q)

    def near(p, q):
        return jnp.where(even, p, pltpu.roll(q, 32, axis)), jnp.where(even, pltpu.roll(p, 96, axis), q)

    a, c = far(a, c)
    b, d = far(b, d)
    a, b = near(a, b)
    c, d = near(c, d)
    return a, b, c, d


def lanes(t, n=1):
    return slice(t * B, (t + n) * B)


def tiles_forward(c):
    return (0, SHARED + 1) if c % 2 == 0 else (SHARED + 1, TILES)


def tiles_backward(c):
    return (0, SHARED) if c % 2 == 0 else (SHARED, TILES)


def tile_slabs(quad, t):
    if t == SHARED:
        return slice(M - 1, M), slice(4 * quad, 4 * quad + 4)
    half, pair = (0, t) if t < SHARED else (1, t - SHARED - 1)
    first = 4 * quad + 2 * half
    return slice(2 * pair, 2 * pair + 2), slice(first, first + 2)


def kernel(
    classes_x_in, classes_y_in, control, ensemble, innovation, precision, tables_x, tables_y,
    increment, gradient, last, wxt_out,
    classes_x, classes_y, ctl, ens, inn, prec, tx, ty, wxt, wy, send1, recv1, send2, recv2, field, keep, part, rs_recv, mine, half_send, zrecv,
    total, wres, inc, grad,
    in_sem, out_sem, inc_sem, s1_sem, r1_sem, s2_sem, r2_sem, xs_sem, xr_sem, zs_sem, zr_sem, ws_sem, wr_sem, last_sem, group_sem, ready_sem,
):
    me = lax.axis_index("space")
    mem = lax.axis_index("mem")
    my_x = lax.rem(mem, XS)
    my_hi = mem // XS
    base = my_hi * XS
    my_level = lax.rem(my_x, 2)
    my_half = my_x // 2
    other_half = lax.rem(mem + XS, MEM)
    across = base + lax.rem(my_x + 2, XS)

    def piece(ref, c):
        return ref.at[2 * c + my_level, :, pl.ds(pl.multiple_of(my_half * HALF, HALF), HALF)]

    loads = []

    def load(src, dst, pieces=1):
        sem = in_sem.at[len(loads)]
        size = src.shape[0] // pieces
        cuts = [pl.ds(n * size, size) for n in range(pieces)]
        parts = [pltpu.make_async_copy(src.at[cut], dst.at[cut], sem) for cut in cuts]
        loads.append((parts, pltpu.make_async_copy(src, dst, sem)))
        return loads[-1]

    def begin(load):
        for part in load[0]:
            part.start()

    def end(load):
        load[1].wait()

    ld_classes = [load(classes_x_in, classes_x), load(classes_y_in, classes_y)]
    ld_tx = load(tables_x, tx, CLASSES)
    ld_ctl = [load(control.at[:, pl.ds(4 * q, 4)], ctl.at[:, pl.ds(4 * q, 4)], M) for q in range(QUADS)]
    ld_ty = load(tables_y, ty, CLASSES)
    ld_ens = load(ensemble, ens, M)
    ld_obs = [load(piece(innovation, c), inn.at[c]) for c in range(CHUNKS)]
    ld_obs += [load(piece(precision, c), prec.at[c]) for c in range(CHUNKS)]

    urgent = ld_classes + [ld_tx, ld_ctl[0]]
    for item in urgent:
        begin(item)

    barrier = pltpu.get_barrier_semaphore()

    @pl.loop(1, SPACE)
    def _(k):
        pl.semaphore_signal(barrier, inc=1, device_id={"space": lax.rem(me + k, SPACE)}, device_id_type=MESH)

    def x_peer(k):
        return lax.rem(my_x + k, XS)

    leads = me == LEADER
    groups = [base + x_peer(k) for k in range(1, XS)] + [other_half]

    @pl.when(leads)
    def _():
        for group in groups:
            pl.semaphore_signal(barrier, inc=1, device_id={"mem": group}, device_id_type=MESH)

    def enter():
        @pl.when(leads)
        def _():
            pl.semaphore_wait(barrier, SPACE - 1 + len(groups))
            for group in groups:
                pl.semaphore_signal(group_sem, inc=1, device_id={"mem": group}, device_id_type=MESH)

        @pl.when(jnp.logical_not(leads))
        def _():
            pl.semaphore_wait(barrier, SPACE - 1)

    def enter_groups():
        @pl.when(leads)
        def _():
            pl.semaphore_wait(group_sem, len(groups))

            @pl.loop(1, SPACE)
            def _(k):
                pl.semaphore_signal(
                    ready_sem, inc=1, device_id={"space": lax.rem(me + k, SPACE)}, device_id_type=MESH
                )

        @pl.when(jnp.logical_not(leads))
        def _():
            pl.semaphore_wait(ready_sem, 1)

    for item in ld_classes:
        end(item)
    end(ld_tx)
    for b in range(NX // B):
        for j in range(NX // B):
            block = tx[classes_x[b], j - b + 2]
            wxt[lanes(b), lanes(j)] = block.astype(F32).T.astype(BF16)
    wxt_copy = pltpu.make_async_copy(wxt, wxt_out, last_sem.at[0])
    wxt_copy.start()

    def x_filter(c):
        for t in range(*tiles_forward(c)):
            members, levels = tile_slabs(c // 2, t)
            rows = ctl[members, levels].reshape(4 * ROWS, NX)
            out = lax.dot_general(wxt[...], rows, NT, preferred_element_type=F32)
            send1[c // 2, :, :, lanes(t)] = out.reshape(SPACE, COLS, B).astype(BF16)

    def part_of(tiles, c):
        first, last = tiles(c)
        return pl.ds(first * B, (last - first) * B)

    def space_wait(send, recv, tiles, sem, c):
        cut = (c // 2, pl.ds(0, SPACE - 1), slice(None), part_of(tiles, c))
        pltpu.make_async_copy(send.at[cut], recv.at[cut], sem.at[c]).wait()

    own_cut = (QUADS - 1, me, slice(None), part_of(tiles_backward, CHUNKS - 1))
    own_copy = pltpu.make_async_copy(send2.at[own_cut], last.at[me], last_sem.at[1])

    def start2(c):
        q, cut = c // 2, part_of(tiles_backward, c)

        @pl.loop(1, SPACE)
        def _(k):
            d = lax.rem(me + k, SPACE)
            pltpu.make_async_remote_copy(
                src_ref=send2.at[q, d, :, cut],
                dst_ref=last.at[me] if c == CHUNKS - 1 else recv2.at[q, me, :, cut],
                send_sem=s2_sem.at[c], recv_sem=r2_sem.at[c],
                device_id={"space": d}, device_id_type=MESH,
            ).start()

        if c == CHUNKS - 1:
            own_copy.start()
        else:
            recv2[q, me, :, cut] = send2[q, me, :, cut]

    def start1(c, batch):
        q, cut = c // 2, part_of(tiles_forward, c)

        @pl.loop(1 if batch == 0 else 0, SPACE // BATCHES)
        def _(t):
            d = lax.rem(me + BATCHES * t + batch, SPACE)
            pltpu.make_async_remote_copy(
                src_ref=send1.at[q, d, :, cut], dst_ref=recv1.at[q, me, :, cut],
                send_sem=s1_sem.at[c, batch], recv_sem=r1_sem.at[c],
                device_id={"space": d}, device_id_type=MESH,
            ).start()

        if batch == 0:
            recv1[q, me, :, cut] = send1[q, me, :, cut]

    def sent1(c, batch):
        n = SPACE // BATCHES - (batch == 0)
        cut = (c // 2, pl.ds(0, n), slice(None), part_of(tiles_forward, c))
        pltpu.make_async_copy(send1.at[cut], recv1.at[cut], s1_sem.at[c, batch]).wait()

    def follow1(c, batch):
        sent1(c - 1, batch)
        start1(c, batch)

    def got1(c):
        space_wait(send1, recv1, tiles_forward, r1_sem, c)

    def sent2(c):
        space_wait(send2, recv2, tiles_backward, s2_sem, c)

    def got2(c):
        if c == CHUNKS - 1:
            cut = pl.ds(0, SPACE - 1)
            pltpu.make_async_copy(last.at[cut], last.at[cut], r2_sem.at[c]).wait()
        else:
            space_wait(send2, recv2, tiles_backward, r2_sem, c)

    def band(s):
        return max(0, 2 * s - 2) * B, min(NB, 2 * s + 4) * B

    def to_fields(c):
        q = c // 2
        for t in range(*tiles_forward(c)):
            block = recv1[q, :, :, lanes(t)].astype(F32).reshape(NB, 4, COLS, B)
            out = swap_groups([block[:, j] for j in range(4)])
            for b in range(NB):
                tile = jnp.concatenate([out[i][b] for i in range(4)], axis=0).astype(BF16)
                if t == SHARED:
                    field[c, 2 * PAIRS * 16 :, lanes(b)] = tile[:16]
                    field[c + 1, 2 * PAIRS * 16 :, lanes(b)] = tile[16:]
                else:
                    row = (t if t < SHARED else t - SHARED - 1) * 32
                    field[c, row : row + 32, lanes(b)] = tile

    def member(c, m, cols):
        return ens[m, 2 * c : 2 * c + 2, :, cols].astype(F32).reshape(2 * COLS, -1)

    def forward(c):
        to_fields(c)
        for s in range(NB // 2):
            lo, hi = band(s)
            cols = lanes(2 * s, 2)
            out = jnp.dot(field[c, :, lo:hi], wy[lo:hi, cols], preferred_element_type=F32)
            acc = member(c, 0, cols) * out[:16]
            for m in range(1, M):
                acc = acc + member(c, m, cols) * out[16 * m : 16 * (m + 1)]
            for level in range(2):
                part[c, 2 * (s // 2) + level, :, lanes(2 * (s % 2), 2)] = acc[COLS * level : COLS * (level + 1)]
        for k in range(1, XS):
            p = x_peer(k)
            pltpu.make_async_remote_copy(
                src_ref=part.at[c, p], dst_ref=rs_recv.at[c, my_x], send_sem=xs_sem.at[c], recv_sem=xr_sem.at[c],
                device_id={"mem": base + p}, device_id_type=MESH,
            ).start()
        rs_recv[c, my_x] = part[c, my_x]

    def peers_wait(ref, sem, c):
        cut = (c, pl.ds(0, XS - 1))
        pltpu.make_async_copy(ref.at[cut], ref.at[cut], sem.at[c]).wait()

    def half_copy(c):
        return pltpu.make_async_remote_copy(
            src_ref=half_send.at[c], dst_ref=zrecv.at[c], send_sem=zs_sem.at[c], recv_sem=zr_sem.at[c],
            device_id={"mem": other_half}, device_id_type=MESH,
        )

    def sum_x(c):
        peers_wait(rs_recv, xr_sem, c)
        mine[c] = (rs_recv[c, 0] + rs_recv[c, 1]) + (rs_recv[c, 2] + rs_recv[c, 3])
        half_send[c] = mine[c].astype(BF16)
        half_copy(c).start()

    def weigh(c):
        half_copy(c).wait_recv()
        total[c] = mine[c] + zrecv[c].astype(F32)
        wres[c, my_x] = (prec[c] * (total[c] - inn[c])).astype(BF16)
        for k in range(1, XS):
            pltpu.make_async_remote_copy(
                src_ref=wres.at[c, my_x], dst_ref=wres.at[c, my_x], send_sem=ws_sem.at[c], recv_sem=wr_sem.at[c],
                device_id={"mem": base + x_peer(k)}, device_id_type=MESH,
            ).start()

    def backward(c):
        q, odd = c // 2, c % 2
        peers_wait(wres, wr_sem, c)
        weight = jnp.concatenate(
            [
                jnp.concatenate([wres[c, level].astype(F32), wres[c, 2 + level].astype(F32)], axis=1)
                for level in range(2)
            ],
            axis=0,
        )
        for m in range(M):
            field[c, 16 * m : 16 * (m + 1)] = (member(c, m, slice(None)) * weight).astype(BF16)
        for s in range(NB // 2):
            lo, hi = band(s)
            out = lax.dot_general(field[c, :, lo:hi], wy[lanes(2 * s, 2), lo:hi], NT, preferred_element_type=F32)
            for b in (2 * s, 2 * s + 1):
                cols = lanes(b - 2 * s)
                groups = [
                    (pair + odd * (SHARED + 1), out[32 * pair : 32 * (pair + 1), cols]) for pair in range(PAIRS)
                ]
                last = out[32 * PAIRS :, cols]
                if odd:
                    groups.append((SHARED, jnp.concatenate([keep[:, lanes(b)], last], axis=0)))
                else:
                    keep[:, lanes(b)] = last
                for t, rows in groups:
                    rows = rows.reshape(4, COLS, B)
                    swapped = swap_groups([rows[i] for i in range(4)])
                    for j in range(4):
                        send2[q, 4 * b + j, :, lanes(t)] = swapped[j].astype(BF16)
        start2(c)

    def out_copies(c):
        pairs = (slice(0, 2 * PAIRS), slice(2 * c, 2 * c + 2))
        copies = [pltpu.make_async_copy(grad.at[pairs], gradient.at[pairs], out_sem.at[c])]
        if c % 2:
            shared = (slice(M - 1, M), slice(2 * c - 2, 2 * c + 2))
            copies.append(pltpu.make_async_copy(grad.at[shared], gradient.at[shared], out_sem.at[CHUNKS + c // 2]))
        return copies

    def finish(c):
        got2(c)
        for t in range(*tiles_backward(c)):
            slabs = tile_slabs(c // 2, t)
            cols = recv2[c // 2, :, :, lanes(t)].astype(F32).reshape(NX, B).astype(BF16)
            out = lax.dot_general(cols, wxt[...], TN, preferred_element_type=F32)
            old = ctl[slabs]
            grad[slabs] = (old.astype(F32) + out.reshape(old.shape)).astype(BF16)
        for copy in out_copies(c):
            copy.start()

    end(ld_ctl[0])
    for item in loads:
        if all(item is not other for other in urgent):
            begin(item)
    x_filter(0)
    enter()
    for batch in range(BATCHES):
        start1(0, batch)
    x_filter(1)
    end(ld_ctl[1])
    follow1(1, 0)
    x_filter(2)
    follow1(1, 1)
    x_filter(3)
    enter_groups()

    end(ld_ty)
    for b in range(NB):
        for j in range(NB):
            if abs(j - b) <= 2:
                wy[lanes(j), lanes(b)] = ty[classes_y[b], j - b + 2]
            elif abs(j - b) == 3:
                wy[lanes(j), lanes(b)] = jnp.zeros((B, B), BF16)
    end(ld_ens)
    for item in ld_obs:
        end(item)

    follow1(1, 2)
    follow1(1, 3)
    got1(0)
    forward(0)
    for batch in range(BATCHES):
        follow1(2, batch)
    got1(1)
    forward(1)
    sum_x(0)
    for batch in range(BATCHES):
        follow1(3, batch)
    got1(2)
    forward(2)
    sum_x(1)
    weigh(0)
    got1(3)
    forward(3)
    sum_x(2)
    backward(0)
    weigh(1)
    sum_x(3)
    backward(1)
    weigh(2)
    backward(2)
    weigh(3)

    kept = pl.ds(pl.multiple_of(my_half * HALF, HALF), HALF)
    inc[0, :, kept] = total[2 * my_hi + my_half]
    given = pltpu.make_async_remote_copy(
        src_ref=total.at[2 * my_hi + 1 - my_half], dst_ref=inc.at[0, :, kept],
        send_sem=inc_sem.at[0], recv_sem=inc_sem.at[1], device_id={"mem": across}, device_id_type=MESH,
    )
    given.start()
    backward(3)
    finish(0)
    finish(1)
    given.wait()
    inc_copy = pltpu.make_async_copy(inc, increment, out_sem.at[CHUNKS + QUADS])
    inc_copy.start()
    finish(2)
    for c in range(CHUNKS):
        peers_wait(rs_recv, xs_sem, c)
        half_copy(c).wait_send()
        peers_wait(wres, ws_sem, c)
        sent2(c)
    for batch in range(BATCHES):
        sent1(CHUNKS - 1, batch)
    own_copy.wait()
    wxt_copy.wait()
    inc_copy.wait()
    for c in range(CHUNKS - 1):
        for copy in out_copies(c):
            copy.wait()
    got2(CHUNKS - 1)


def write_out(inc_in, grad_in, last_in, wxt_in, control, increment, gradient, inc, grad, last, wxt, ctl, sem):
    pairs = (slice(0, 2 * PAIRS), slice(LEVELS - 2, LEVELS))
    shared = (slice(M - 1, M), slice(LEVELS - 4, LEVELS))
    needs = [
        pltpu.make_async_copy(last_in, last, sem.at[2, 0]),
        pltpu.make_async_copy(wxt_in, wxt, sem.at[2, 1]),
        pltpu.make_async_copy(control.at[pairs], ctl.at[pairs], sem.at[2, 2]),
        pltpu.make_async_copy(control.at[shared], ctl.at[shared], sem.at[2, 3]),
    ]
    cuts = [(m, slice(0, LEVELS - 4 if m == M - 1 else LEVELS - 2)) for m in range(M)]
    copies = [(inc_in, inc, increment)] + [(grad_in.at[cut], grad.at[cut], gradient.at[cut]) for cut in cuts]
    loads = [pltpu.make_async_copy(src, via, sem.at[0, n]) for n, (src, via, _) in enumerate(copies)]
    stores = [pltpu.make_async_copy(via, dst, sem.at[1, n]) for n, (_, via, dst) in enumerate(copies)]
    for copy in needs + loads:
        copy.start()
    for copy in needs:
        copy.wait()
    for t in range(SHARED, TILES):
        slabs = tile_slabs(QUADS - 1, t)
        cols = last[:, :, lanes(t - SHARED)].astype(F32).reshape(NX, B).astype(BF16)
        out = lax.dot_general(cols, wxt[...], TN, preferred_element_type=F32)
        old = ctl[slabs]
        grad[slabs] = (old.astype(F32) + out.reshape(old.shape)).astype(BF16)
        ends = pltpu.make_async_copy(grad.at[slabs], gradient.at[slabs], sem.at[3, t - SHARED])
        ends.start()
        stores.append(ends)
    for n, load in enumerate(loads):
        load.wait()
        stores[n].start()
    for store in stores:
        store.wait()


def per_device(control, ensemble, innovation, precision_obs, classes_x, classes_y, tables_x, tables_y):
    any_space = pl.BlockSpec(memory_space=pl.ANY)
    dma = pltpu.SemaphoreType.DMA
    message = pltpu.VMEM((QUADS, SPACE, COLS, TILES * B), BF16)
    sums = pltpu.VMEM((CHUNKS, XS, COLS, HALF), F32)
    piece = pltpu.VMEM((CHUNKS, COLS, HALF), F32)
    shapes = (
        jax.ShapeDtypeStruct((1, COLS, NY), F32),
        jax.ShapeDtypeStruct((M, LEVELS, ROWS, NX), BF16),
    )
    results = pl.pallas_call(
        kernel,
        out_shape=shapes
        + (
            jax.ShapeDtypeStruct((SPACE, COLS, (TILES - SHARED) * B), BF16),
            jax.ShapeDtypeStruct((NX, NX), BF16),
        ),
        in_specs=[any_space] * 8,
        out_specs=(any_space,) * 4,
        scratch_shapes=[
            pltpu.SMEM(classes_x.shape, jnp.int32),
            pltpu.SMEM(classes_y.shape, jnp.int32),
            pltpu.VMEM((M, LEVELS, ROWS, NX), BF16),
            pltpu.VMEM((M, LEVELS, COLS, NY), BF16),
            piece,
            piece,
            pltpu.VMEM(tables_x.shape, BF16),
            pltpu.VMEM(tables_y.shape, BF16),
            pltpu.VMEM((NX, NX), BF16),
            pltpu.VMEM((NY, NY), BF16),
            message,
            message,
            message,
            message,
            pltpu.VMEM((CHUNKS, FIELD, NY), BF16),
            pltpu.VMEM((2 * COLS, NY), F32),
            sums,
            sums,
            piece,
            pltpu.VMEM((CHUNKS, COLS, HALF), BF16),
            pltpu.VMEM((CHUNKS, COLS, HALF), BF16),
            piece,
            pltpu.VMEM((CHUNKS, XS, COLS, HALF), BF16),
            pltpu.VMEM((1, COLS, NY), F32),
            pltpu.VMEM((M, LEVELS, ROWS, NX), BF16),
            dma((7 + 2 * CHUNKS,)),
            dma((CHUNKS + QUADS + 1,)),
            dma((2,)),
        ]
        + [dma((CHUNKS, BATCHES))]
        + [dma((CHUNKS,))] * 9
        + [dma((2,))]
        + [pltpu.SemaphoreType.REGULAR] * 2,
        compiler_params=pltpu.CompilerParams(
            collective_id=0, has_side_effects=True, vmem_limit_bytes=63 << 20
        ),
        name="hybrid_envar",
    )(classes_x, classes_y, control, ensemble, innovation, precision_obs, tables_x, tables_y)
    return pl.pallas_call(
        write_out,
        out_shape=shapes,
        in_specs=[any_space] * 5,
        out_specs=(any_space,) * 2,
        scratch_shapes=[pltpu.VMEM(shape.shape, shape.dtype) for shape in shapes]
        + [
            pltpu.VMEM((SPACE, COLS, (TILES - SHARED) * B), BF16),
            pltpu.VMEM((NX, NX), BF16),
            pltpu.VMEM((M, LEVELS, ROWS, NX), BF16),
            dma((4, M + 1)),
        ],
        compiler_params=pltpu.CompilerParams(vmem_limit_bytes=63 << 20),
        name="write_out",
    )(*results, control)


def solution(mesh):
    in_specs = (
        P("mem", None, "space", None),
        P("mem", None, "space", None),
        P(None, "space", None),
        P(None, "space", None),
        P(),
        P(),
        P(),
        P(),
    )
    out_specs = (P("mem", "space", None), P("mem", None, "space", None))
    return jax.shard_map(
        per_device, mesh=mesh, in_specs=in_specs, out_specs=out_specs, check_vma=False
    )
```

```python
import jax
import jax.numpy as jnp
from jax import lax
from jax.experimental import pallas as pl
from jax.experimental.pallas import tpu as pltpu
from jax.sharding import PartitionSpec as P

MESH = pl.DeviceIdType.MESH
F32 = jnp.float32
BF16 = jnp.bfloat16
NT = (((1,), (1,)), ((), ()))
TN = (((0,), (0,)), ((), ()))

SPACE = 32
LEADER = 2
MEM = 8
XS = 4
M = 7
PAIRS = M // 2
LEVELS = 8
CLASSES = 8
CHUNKS = 4
BATCHES = 4
QUADS = CHUNKS // 2
ROWS = 32
COLS = 8
NX = 256
NY = 1024
B = 128
NB = NY // B
HALF = NY // 2
TILES = 2 * PAIRS + 1
SHARED = PAIRS
FIELD = M * 2 * COLS


def swap_groups(tiles):
    a, b, c, d = tiles
    axis = a.ndim - 1
    lane = lax.broadcasted_iota(jnp.int32, a.shape, axis)
    low = lane < 64
    even = lax.rem(lane, 64) < 32

    def far(p, q):
        return jnp.where(low, p, pltpu.roll(q, 64, axis)), jnp.where(low, pltpu.roll(p, 64, axis), q)

    def near(p, q):
        return jnp.where(even, p, pltpu.roll(q, 32, axis)), jnp.where(even, pltpu.roll(p, 96, axis), q)

    a, c = far(a, c)
    b, d = far(b, d)
    a, b = near(a, b)
    c, d = near(c, d)
    return a, b, c, d


def lanes(t, n=1):
    return slice(t * B, (t + n) * B)


def tiles_forward(c):
    return (0, SHARED + 1) if c % 2 == 0 else (SHARED + 1, TILES)


def tiles_backward(c):
    return (0, SHARED) if c % 2 == 0 else (SHARED, TILES)


def tile_slabs(quad, t):
    if t == SHARED:
        return slice(M - 1, M), slice(4 * quad, 4 * quad + 4)
    half, pair = (0, t) if t < SHARED else (1, t - SHARED - 1)
    first = 4 * quad + 2 * half
    return slice(2 * pair, 2 * pair + 2), slice(first, first + 2)


def kernel(
    classes_x_in, classes_y_in, control, ensemble, innovation, precision, tables_x, tables_y,
    increment, gradient, last, wxt_out,
    classes_x, classes_y, ctl, ens, inn, prec, tx, ty, wxt, wy, send1, recv1, send2, recv2, field, keep, part, rs_recv, mine, half_send, zrecv,
    total, wres, inc, grad,
    in_sem, out_sem, inc_sem, s1_sem, r1_sem, s2_sem, r2_sem, xs_sem, xr_sem, zs_sem, zr_sem, ws_sem, wr_sem, last_sem, group_sem, ready_sem,
):
    me = lax.axis_index("space")
    mem = lax.axis_index("mem")
    my_x = lax.rem(mem, XS)
    my_hi = mem // XS
    base = my_hi * XS
    my_level = lax.rem(my_x, 2)
    my_half = my_x // 2
    other_half = lax.rem(mem + XS, MEM)
    across = base + lax.rem(my_x + 2, XS)

    def piece(ref, c):
        return ref.at[2 * c + my_level, :, pl.ds(pl.multiple_of(my_half * HALF, HALF), HALF)]

    loads = []

    def load(src, dst, pieces=1):
        sem = in_sem.at[len(loads)]
        size = src.shape[0] // pieces
        cuts = [pl.ds(n * size, size) for n in range(pieces)]
        parts = [pltpu.make_async_copy(src.at[cut], dst.at[cut], sem) for cut in cuts]
        loads.append((parts, pltpu.make_async_copy(src, dst, sem)))
        return loads[-1]

    def begin(load):
        for part in load[0]:
            part.start()

    def end(load):
        load[1].wait()

    ld_classes = [load(classes_x_in, classes_x), load(classes_y_in, classes_y)]
    ld_tx = load(tables_x, tx, CLASSES)
    ld_ctl = [load(control.at[:, pl.ds(4 * q, 4)], ctl.at[:, pl.ds(4 * q, 4)], M) for q in range(QUADS)]
    ld_ty = load(tables_y, ty, CLASSES)
    ld_ens = load(ensemble, ens, M)
    ld_obs = [load(piece(innovation, c), inn.at[c]) for c in range(CHUNKS)]
    ld_obs += [load(piece(precision, c), prec.at[c]) for c in range(CHUNKS)]

    barrier = pltpu.get_barrier_semaphore()

    @pl.loop(1, SPACE)
    def _(k):
        pl.semaphore_signal(barrier, inc=1, device_id={"space": lax.rem(me + k, SPACE)}, device_id_type=MESH)

    def x_peer(k):
        return lax.rem(my_x + k, XS)

    leads = me == LEADER
    groups = [base + x_peer(k) for k in range(1, XS)] + [other_half]

    @pl.when(leads)
    def _():
        for group in groups:
            pl.semaphore_signal(barrier, inc=1, device_id={"mem": group}, device_id_type=MESH)

    urgent = ld_classes + [ld_tx, ld_ctl[0]]
    for item in urgent:
        begin(item)

    def enter():
        @pl.when(leads)
        def _():
            pl.semaphore_wait(barrier, SPACE - 1 + len(groups))
            for group in groups:
                pl.semaphore_signal(group_sem, inc=1, device_id={"mem": group}, device_id_type=MESH)

        @pl.when(jnp.logical_not(leads))
        def _():
            pl.semaphore_wait(barrier, SPACE - 1)

    def enter_groups():
        @pl.when(leads)
        def _():
            pl.semaphore_wait(group_sem, len(groups))

            @pl.loop(1, SPACE)
            def _(k):
                pl.semaphore_signal(
                    ready_sem, inc=1, device_id={"space": lax.rem(me + k, SPACE)}, device_id_type=MESH
                )

        @pl.when(jnp.logical_not(leads))
        def _():
            pl.semaphore_wait(ready_sem, 1)

    for item in ld_classes:
        end(item)
    end(ld_tx)
    for b in range(NX // B):
        for j in range(NX // B):
            block = tx[classes_x[b], j - b + 2]
            wxt[lanes(b), lanes(j)] = block.astype(F32).T.astype(BF16)
    wxt_copy = pltpu.make_async_copy(wxt, wxt_out, last_sem.at[0])
    wxt_copy.start()

    def x_filter(c):
        for t in range(*tiles_forward(c)):
            members, levels = tile_slabs(c // 2, t)
            rows = ctl[members, levels].reshape(4 * ROWS, NX)
            out = lax.dot_general(wxt[...], rows, NT, preferred_element_type=F32)
            send1[c // 2, :, :, lanes(t)] = out.reshape(SPACE, COLS, B).astype(BF16)

    def part_of(tiles, c):
        first, last = tiles(c)
        return pl.ds(first * B, (last - first) * B)

    def space_wait(send, recv, tiles, sem, c):
        cut = (c // 2, pl.ds(0, SPACE - 1), slice(None), part_of(tiles, c))
        pltpu.make_async_copy(send.at[cut], recv.at[cut], sem.at[c]).wait()

    own_cut = (QUADS - 1, me, slice(None), part_of(tiles_backward, CHUNKS - 1))
    own_copy = pltpu.make_async_copy(send2.at[own_cut], last.at[me], last_sem.at[1])

    def start2(c):
        q, cut = c // 2, part_of(tiles_backward, c)

        @pl.loop(1, SPACE)
        def _(k):
            d = lax.rem(me + k, SPACE)
            pltpu.make_async_remote_copy(
                src_ref=send2.at[q, d, :, cut],
                dst_ref=last.at[me] if c == CHUNKS - 1 else recv2.at[q, me, :, cut],
                send_sem=s2_sem.at[c], recv_sem=r2_sem.at[c],
                device_id={"space": d}, device_id_type=MESH,
            ).start()

        if c == CHUNKS - 1:
            own_copy.start()
        else:
            recv2[q, me, :, cut] = send2[q, me, :, cut]

    def start1(c, batch):
        q, cut = c // 2, part_of(tiles_forward, c)

        @pl.loop(1 if batch == 0 else 0, SPACE // BATCHES)
        def _(t):
            d = lax.rem(me + BATCHES * t + batch, SPACE)
            pltpu.make_async_remote_copy(
                src_ref=send1.at[q, d, :, cut], dst_ref=recv1.at[q, me, :, cut],
                send_sem=s1_sem.at[c, batch], recv_sem=r1_sem.at[c],
                device_id={"space": d}, device_id_type=MESH,
            ).start()

        if batch == 0:
            recv1[q, me, :, cut] = send1[q, me, :, cut]

    def sent1(c, batch):
        n = SPACE // BATCHES - (batch == 0)
        cut = (c // 2, pl.ds(0, n), slice(None), part_of(tiles_forward, c))
        pltpu.make_async_copy(send1.at[cut], recv1.at[cut], s1_sem.at[c, batch]).wait()

    def follow1(c, batch):
        sent1(c - 1, batch)
        start1(c, batch)

    def got1(c):
        space_wait(send1, recv1, tiles_forward, r1_sem, c)

    def sent2(c):
        space_wait(send2, recv2, tiles_backward, s2_sem, c)

    def got2(c):
        if c == CHUNKS - 1:
            cut = pl.ds(0, SPACE - 1)
            pltpu.make_async_copy(last.at[cut], last.at[cut], r2_sem.at[c]).wait()
        else:
            space_wait(send2, recv2, tiles_backward, r2_sem, c)

    def band(s):
        return max(0, 2 * s - 2) * B, min(NB, 2 * s + 4) * B

    def to_fields(c):
        q = c // 2
        for t in range(*tiles_forward(c)):
            block = recv1[q, :, :, lanes(t)].astype(F32).reshape(NB, 4, COLS, B)
            out = swap_groups([block[:, j] for j in range(4)])
            for b in range(NB):
                tile = jnp.concatenate([out[i][b] for i in range(4)], axis=0).astype(BF16)
                if t == SHARED:
                    field[c, 2 * PAIRS * 16 :, lanes(b)] = tile[:16]
                    field[c + 1, 2 * PAIRS * 16 :, lanes(b)] = tile[16:]
                else:
                    row = (t if t < SHARED else t - SHARED - 1) * 32
                    field[c, row : row + 32, lanes(b)] = tile

    def member(c, m, cols):
        return ens[m, 2 * c : 2 * c + 2, :, cols].astype(F32).reshape(2 * COLS, -1)

    def forward(c):
        to_fields(c)
        for s in range(NB // 2):
            lo, hi = band(s)
            cols = lanes(2 * s, 2)
            out = jnp.dot(field[c, :, lo:hi], wy[lo:hi, cols], preferred_element_type=F32)
            acc = member(c, 0, cols) * out[:16]
            for m in range(1, M):
                acc = acc + member(c, m, cols) * out[16 * m : 16 * (m + 1)]
            for level in range(2):
                part[c, 2 * (s // 2) + level, :, lanes(2 * (s % 2), 2)] = acc[COLS * level : COLS * (level + 1)]
        for k in range(1, XS):
            p = x_peer(k)
            pltpu.make_async_remote_copy(
                src_ref=part.at[c, p], dst_ref=rs_recv.at[c, my_x], send_sem=xs_sem.at[c], recv_sem=xr_sem.at[c],
                device_id={"mem": base + p}, device_id_type=MESH,
            ).start()
        rs_recv[c, my_x] = part[c, my_x]

    def peers_wait(ref, sem, c):
        cut = (c, pl.ds(0, XS - 1))
        pltpu.make_async_copy(ref.at[cut], ref.at[cut], sem.at[c]).wait()

    def half_copy(c):
        return pltpu.make_async_remote_copy(
            src_ref=half_send.at[c], dst_ref=zrecv.at[c], send_sem=zs_sem.at[c], recv_sem=zr_sem.at[c],
            device_id={"mem": other_half}, device_id_type=MESH,
        )

    def sum_x(c):
        peers_wait(rs_recv, xr_sem, c)
        mine[c] = (rs_recv[c, 0] + rs_recv[c, 1]) + (rs_recv[c, 2] + rs_recv[c, 3])
        half_send[c] = mine[c].astype(BF16)
        half_copy(c).start()

    def weigh(c):
        half_copy(c).wait_recv()
        total[c] = mine[c] + zrecv[c].astype(F32)
        wres[c, my_x] = (prec[c] * (total[c] - inn[c])).astype(BF16)
        for k in range(1, XS):
            pltpu.make_async_remote_copy(
                src_ref=wres.at[c, my_x], dst_ref=wres.at[c, my_x], send_sem=ws_sem.at[c], recv_sem=wr_sem.at[c],
                device_id={"mem": base + x_peer(k)}, device_id_type=MESH,
            ).start()

    def backward(c):
        q, odd = c // 2, c % 2
        peers_wait(wres, wr_sem, c)
        weight = jnp.concatenate(
            [
                jnp.concatenate([wres[c, level].astype(F32), wres[c, 2 + level].astype(F32)], axis=1)
                for level in range(2)
            ],
            axis=0,
        )
        for m in range(M):
            field[c, 16 * m : 16 * (m + 1)] = (member(c, m, slice(None)) * weight).astype(BF16)
        for s in range(NB // 2):
            lo, hi = band(s)
            out = lax.dot_general(field[c, :, lo:hi], wy[lanes(2 * s, 2), lo:hi], NT, preferred_element_type=F32)
            for b in (2 * s, 2 * s + 1):
                cols = lanes(b - 2 * s)
                groups = [
                    (pair + odd * (SHARED + 1), out[32 * pair : 32 * (pair + 1), cols]) for pair in range(PAIRS)
                ]
                last = out[32 * PAIRS :, cols]
                if odd:
                    groups.append((SHARED, jnp.concatenate([keep[:, lanes(b)], last], axis=0)))
                else:
                    keep[:, lanes(b)] = last
                for t, rows in groups:
                    rows = rows.reshape(4, COLS, B)
                    swapped = swap_groups([rows[i] for i in range(4)])
                    for j in range(4):
                        send2[q, 4 * b + j, :, lanes(t)] = swapped[j].astype(BF16)
        start2(c)

    def out_copies(c):
        pairs = (slice(0, 2 * PAIRS), slice(2 * c, 2 * c + 2))
        copies = [pltpu.make_async_copy(grad.at[pairs], gradient.at[pairs], out_sem.at[c])]
        if c % 2:
            shared = (slice(M - 1, M), slice(2 * c - 2, 2 * c + 2))
            copies.append(pltpu.make_async_copy(grad.at[shared], gradient.at[shared], out_sem.at[CHUNKS + c // 2]))
        return copies

    def finish(c):
        got2(c)
        for t in range(*tiles_backward(c)):
            slabs = tile_slabs(c // 2, t)
            cols = recv2[c // 2, :, :, lanes(t)].astype(F32).reshape(NX, B).astype(BF16)
            out = lax.dot_general(cols, wxt[...], TN, preferred_element_type=F32)
            old = ctl[slabs]
            grad[slabs] = (old.astype(F32) + out.reshape(old.shape)).astype(BF16)
        for copy in out_copies(c):
            copy.start()

    end(ld_ctl[0])
    for item in loads:
        if all(item is not other for other in urgent):
            begin(item)
    x_filter(0)
    enter()
    for batch in range(BATCHES):
        start1(0, batch)
    x_filter(1)
    end(ld_ctl[1])
    follow1(1, 0)
    x_filter(2)
    follow1(1, 1)
    x_filter(3)
    enter_groups()

    end(ld_ty)
    for b in range(NB):
        for j in range(NB):
            if abs(j - b) <= 2:
                wy[lanes(j), lanes(b)] = ty[classes_y[b], j - b + 2]
            elif abs(j - b) == 3:
                wy[lanes(j), lanes(b)] = jnp.zeros((B, B), BF16)
    end(ld_ens)
    for item in ld_obs:
        end(item)

    follow1(1, 2)
    follow1(1, 3)
    got1(0)
    forward(0)
    for batch in range(BATCHES):
        follow1(2, batch)
    got1(1)
    forward(1)
    sum_x(0)
    for batch in range(BATCHES):
        follow1(3, batch)
    got1(2)
    forward(2)
    sum_x(1)
    weigh(0)
    got1(3)
    forward(3)
    sum_x(2)
    backward(0)
    sum_x(3)
    weigh(1)
    backward(1)
    weigh(2)
    backward(2)
    finish(0)
    weigh(3)

    kept = pl.ds(pl.multiple_of(my_half * HALF, HALF), HALF)
    inc[0, :, kept] = total[2 * my_hi + my_half]
    given = pltpu.make_async_remote_copy(
        src_ref=total.at[2 * my_hi + 1 - my_half], dst_ref=inc.at[0, :, kept],
        send_sem=inc_sem.at[0], recv_sem=inc_sem.at[1], device_id={"mem": across}, device_id_type=MESH,
    )
    given.start()
    backward(3)
    finish(1)
    given.wait()
    inc_copy = pltpu.make_async_copy(inc, increment, out_sem.at[CHUNKS + QUADS])
    inc_copy.start()
    finish(2)
    for c in range(CHUNKS):
        peers_wait(rs_recv, xs_sem, c)
        half_copy(c).wait_send()
        peers_wait(wres, ws_sem, c)
        sent2(c)
    for batch in range(BATCHES):
        sent1(CHUNKS - 1, batch)
    own_copy.wait()
    wxt_copy.wait()
    inc_copy.wait()
    for c in range(CHUNKS - 1):
        for copy in out_copies(c):
            copy.wait()
    got2(CHUNKS - 1)


def write_out(inc_in, grad_in, last_in, wxt_in, control, increment, gradient, inc, grad, last, wxt, ctl, sem):
    pairs = (slice(0, 2 * PAIRS), slice(LEVELS - 2, LEVELS))
    shared = (slice(M - 1, M), slice(LEVELS - 4, LEVELS))
    needs = [
        pltpu.make_async_copy(last_in, last, sem.at[2, 0]),
        pltpu.make_async_copy(wxt_in, wxt, sem.at[2, 1]),
        pltpu.make_async_copy(control.at[pairs], ctl.at[pairs], sem.at[2, 2]),
        pltpu.make_async_copy(control.at[shared], ctl.at[shared], sem.at[2, 3]),
    ]
    cuts = [(m, slice(0, LEVELS - 4 if m == M - 1 else LEVELS - 2)) for m in range(M)]
    copies = [(inc_in, inc, increment)] + [(grad_in.at[cut], grad.at[cut], gradient.at[cut]) for cut in cuts]
    loads = [pltpu.make_async_copy(src, via, sem.at[0, n]) for n, (src, via, _) in enumerate(copies)]
    stores = [pltpu.make_async_copy(via, dst, sem.at[1, n]) for n, (_, via, dst) in enumerate(copies)]
    for copy in needs + loads:
        copy.start()
    for copy in needs:
        copy.wait()
    for t in range(SHARED, TILES):
        slabs = tile_slabs(QUADS - 1, t)
        cols = last[:, :, lanes(t - SHARED)].astype(F32).reshape(NX, B).astype(BF16)
        out = lax.dot_general(cols, wxt[...], TN, preferred_element_type=F32)
        old = ctl[slabs]
        grad[slabs] = (old.astype(F32) + out.reshape(old.shape)).astype(BF16)
        ends = pltpu.make_async_copy(grad.at[slabs], gradient.at[slabs], sem.at[3, t - SHARED])
        ends.start()
        stores.append(ends)
    for n, load in enumerate(loads):
        load.wait()
        stores[n].start()
    for store in stores:
        store.wait()


def per_device(control, ensemble, innovation, precision_obs, classes_x, classes_y, tables_x, tables_y):
    any_space = pl.BlockSpec(memory_space=pl.ANY)
    dma = pltpu.SemaphoreType.DMA
    message = pltpu.VMEM((QUADS, SPACE, COLS, TILES * B), BF16)
    sums = pltpu.VMEM((CHUNKS, XS, COLS, HALF), F32)
    piece = pltpu.VMEM((CHUNKS, COLS, HALF), F32)
    shapes = (
        jax.ShapeDtypeStruct((1, COLS, NY), F32),
        jax.ShapeDtypeStruct((M, LEVELS, ROWS, NX), BF16),
    )
    results = pl.pallas_call(
        kernel,
        out_shape=shapes
        + (
            jax.ShapeDtypeStruct((SPACE, COLS, (TILES - SHARED) * B), BF16),
            jax.ShapeDtypeStruct((NX, NX), BF16),
        ),
        in_specs=[any_space] * 8,
        out_specs=(any_space,) * 4,
        scratch_shapes=[
            pltpu.SMEM(classes_x.shape, jnp.int32),
            pltpu.SMEM(classes_y.shape, jnp.int32),
            pltpu.VMEM((M, LEVELS, ROWS, NX), BF16),
            pltpu.VMEM((M, LEVELS, COLS, NY), BF16),
            piece,
            piece,
            pltpu.VMEM(tables_x.shape, BF16),
            pltpu.VMEM(tables_y.shape, BF16),
            pltpu.VMEM((NX, NX), BF16),
            pltpu.VMEM((NY, NY), BF16),
            message,
            message,
            message,
            message,
            pltpu.VMEM((CHUNKS, FIELD, NY), BF16),
            pltpu.VMEM((2 * COLS, NY), F32),
            sums,
            sums,
            piece,
            pltpu.VMEM((CHUNKS, COLS, HALF), BF16),
            pltpu.VMEM((CHUNKS, COLS, HALF), BF16),
            piece,
            pltpu.VMEM((CHUNKS, XS, COLS, HALF), BF16),
            pltpu.VMEM((1, COLS, NY), F32),
            pltpu.VMEM((M, LEVELS, ROWS, NX), BF16),
            dma((7 + 2 * CHUNKS,)),
            dma((CHUNKS + QUADS + 1,)),
            dma((2,)),
        ]
        + [dma((CHUNKS, BATCHES))]
        + [dma((CHUNKS,))] * 9
        + [dma((2,))]
        + [pltpu.SemaphoreType.REGULAR] * 2,
        compiler_params=pltpu.CompilerParams(
            collective_id=0, has_side_effects=True, vmem_limit_bytes=63 << 20
        ),
        name="hybrid_envar",
    )(classes_x, classes_y, control, ensemble, innovation, precision_obs, tables_x, tables_y)
    return pl.pallas_call(
        write_out,
        out_shape=shapes,
        in_specs=[any_space] * 5,
        out_specs=(any_space,) * 2,
        scratch_shapes=[pltpu.VMEM(shape.shape, shape.dtype) for shape in shapes]
        + [
            pltpu.VMEM((SPACE, COLS, (TILES - SHARED) * B), BF16),
            pltpu.VMEM((NX, NX), BF16),
            pltpu.VMEM((M, LEVELS, ROWS, NX), BF16),
            dma((4, M + 1)),
        ],
        compiler_params=pltpu.CompilerParams(vmem_limit_bytes=63 << 20),
        name="write_out",
    )(*results, control)


def solution(mesh):
    in_specs = (
        P("mem", None, "space", None),
        P("mem", None, "space", None),
        P(None, "space", None),
        P(None, "space", None),
        P(),
        P(),
        P(),
        P(),
    )
    out_specs = (P("mem", "space", None), P("mem", None, "space", None))
    return jax.shard_map(
        per_device, mesh=mesh, in_specs=in_specs, out_specs=out_specs, check_vma=False
    )
```
